32 devices in a mesh: groups: 2 (over y), row: 8 (over z, core), col: 2 (over x).
Axes of the slice: x: 2, y: 2, z: 4, core: 2. Of those that a mesh axis runs over, the one named last changes fastest.
Arguments:
- slab: bfloat16 [64, 512, 2048], P(('groups', 'col'), 'row'), parts along dimension 0, may hold values from -32 to 32
- factor_one: bfloat16 [2048, 128], replicated, may hold values from -0.125 to 0.125
- factor_two: bfloat16 [512, 128], P('row'), may hold values from -0.25 to 0.25
Outputs:
- gram: float32 [64, 32], P(('groups', 'col'), 'row'), parts along dimension 0
The draws below stay inside these ranges and needn't reach their ends.
There are 2 independent parts, one for each index of `groups`. The reference program is written for one: setup_inputs(seed, part) draws one part's arguments, and reference() takes and returns one part's arrays. A program takes and returns all parts, laid end to end along the dimension named above; an argument that names none is the same for every part. Nothing has to cross between parts.
All inputs are finite; a program needn't handle non-finite values.
Results may differ from the reference program's by a relative error of at most 0.0003.
Values sent between devices are 32-bit elements; how exact they have to be, the bound alone decides.
No kernel may reach another device: no remote copies, remote signals or barrier semaphores. Data moves between devices by JAX's collectives and lax.ppermute only.
A program may use at most 64 MiB of HBM per device.

```python
import math
import jax
import jax.numpy as jnp
from jax import lax

I1 = 2048
R1 = 128
R2 = 128
I2 = 512
I3 = 32


def draw_slab(key, part):
    key = jax.random.fold_in(key, 7)
    base_key, rough_key, depth_key = jax.random.split(key, 3)
    base = jax.random.truncated_normal(base_key, -4.0, 4.0, (I3, I2, I1), jnp.float32)
    ramp = jnp.exp(math.log(3.0) * jnp.arange(I2, dtype=jnp.float32) / I2)
    rough = jax.random.uniform(rough_key, (I2,), jnp.float32, 0.7, 1.3)
    depth = jnp.exp(jax.random.uniform(depth_key, (I3,), jnp.float32, math.log(0.5), math.log(2.0)))
    scaled = base * (ramp * rough)[None, :, None] * depth[:, None, None]
    return scaled.astype(jnp.bfloat16)


def shard_levels(rng, dims, shards, low, largest):
    level = 1.0
    for dim, blocks in shards:
        heights = jax.random.uniform(jax.random.fold_in(jax.random.fold_in(rng, 6), dim), (blocks,), jnp.float32, low / len(shards), largest / len(shards))
        level = level * jnp.repeat(jnp.exp(heights), dims[dim] // blocks).reshape((-1,) + (1,) * (len(dims) - 1 - dim))
    return level


def normal_values(key, extent, width, most, shards=(), kind=jnp.bfloat16):
    entries = width * jax.random.normal(key, extent, jnp.float32)
    if shards:
        entries = entries * shard_levels(key, extent, shards, -0.22, 0.18)
    return jnp.clip(entries, -most, most).astype(kind)


def setup_inputs(seed: int = 0, part: int = 0) -> dict:
    seeds = jax.random.split(jax.random.key(seed), 4)
    own_keys = jax.random.split(jax.random.fold_in(seeds[3], part), 4)
    return {
        "slab": draw_slab(jax.random.fold_in(jax.random.fold_in(seeds[3], part), 71), part),
        "factor_one": normal_values(seeds[1], (I1, R1), I1 ** -0.5, 0.125),
        "factor_two": normal_values(seeds[2], (I2, R2), I2 ** -0.5, 0.25, ((0, 8),)),
    }


def reference(slab, factor_one, factor_two):
    block = 16 if I3 % 16 == 0 else I3
    pieces = slab.reshape(I3 // block, block, I2, I1)
    one = factor_one.astype(jnp.float32)
    two = factor_two.astype(jnp.float32)

    def project(piece):
        first = jnp.einsum("kji,ir->rkj", piece.astype(jnp.float32), one).astype(jnp.bfloat16)
        return jnp.einsum("rkj,js->rks", first.astype(jnp.float32), two)

    cores = lax.map(project, pieces)
    core = jnp.concatenate([cores[q] for q in range(I3 // block)], axis=1)
    gram = jnp.einsum("rks,rls->kl", core, core, precision=lax.Precision.HIGHEST)
    return gram / float(R1 * R2)
```

```python
import functools

import jax
import jax.numpy as jnp
from jax import lax
from jax.experimental import pallas as pl
from jax.experimental.pallas import tpu as pltpu
from jax.sharding import Mesh, PartitionSpec as P

TILE = 8
CORES = 2
CHUNK = 4


def project_kernel(chunk, slab_ref, one_ref, two_ref, own_ref, other_ref, slab_buf, one_buf, turned, sems):
    depth, width, _ = slab_ref.shape
    chunks = depth // chunk
    half = turned.shape[0] // CORES
    one_copy = pltpu.make_async_copy(one_ref, one_buf, sems.at[chunks])
    one_copy.start()
    copies = []
    for c in range(chunks):
        part = pl.ds(c * chunk, chunk)
        copies.append(pltpu.make_async_copy(slab_ref.at[part], slab_buf.at[part], sems.at[c]))
        copies[-1].start()
    turned[...] = two_ref[...].astype(jnp.float32).T
    core = lax.axis_index("core")
    two_own = turned[pl.ds(pl.multiple_of(core * half, half), half), :].astype(jnp.bfloat16)
    two_other = turned[pl.ds(pl.multiple_of((1 - core) * half, half), half), :].astype(jnp.bfloat16)
    one_copy.wait()
    for c in range(chunks):
        copies[c].wait()
        rows = slab_buf[pl.ds(c * chunk, chunk)].reshape(chunk * width, -1)
        first = jnp.dot(rows, one_buf[...], preferred_element_type=jnp.float32).astype(jnp.bfloat16)
        for q in range(chunk):
            k = c * chunk + q
            piece = first[q * width : (q + 1) * width]
            for two, out in ((two_other, other_ref), (two_own, own_ref)):
                core_part = jnp.dot(two, piece, preferred_element_type=jnp.float32)
                out[:, k] = core_part.reshape(half // TILE, TILE, -1)


def project(slab, factor_one, factor_two):
    depth, width, length = slab.shape
    r1, r2 = factor_one.shape[1], factor_two.shape[1]
    half = r2 // CORES
    chunk = CHUNK if depth % CHUNK == 0 else 1
    out = jax.ShapeDtypeStruct((half // TILE, depth, TILE, r1), jnp.float32)
    return pl.pallas_call(
        functools.partial(project_kernel, chunk),
        out_shape=(out, out),
        in_specs=[
            pl.BlockSpec(memory_space=pl.ANY),
            pl.BlockSpec(memory_space=pl.ANY),
            pl.BlockSpec(memory_space=pltpu.VMEM),
        ],
        out_specs=[pl.BlockSpec(memory_space=pltpu.VMEM)] * 2,
        scratch_shapes=[
            pltpu.VMEM(slab.shape, slab.dtype),
            pltpu.VMEM(factor_one.shape, factor_one.dtype),
            pltpu.VMEM((r2, width), jnp.float32),
            pltpu.SemaphoreType.DMA((depth // chunk + 1,)),
        ],
        compiler_params=pltpu.CompilerParams(vmem_limit_bytes=32 * 2**20),
        cost_estimate=pl.CostEstimate(
            flops=2 * depth * width * r1 * (length + r2),
            bytes_accessed=2 * (slab.size + factor_one.size) + 8 * depth * half * r1,
            transcendentals=0,
        ),
    )(slab, factor_one, factor_two)


def gram_kernel(cols, scale, parts_ref, out_ref, total):
    sources, depth, tile, _ = parts_ref.shape
    for x in range(cols):
        value = parts_ref[x]
        for z in range(1, sources // cols):
            value = value + parts_ref[z * cols + x]
        total[pl.ds(x * depth * tile, depth * tile), :] = value.reshape(depth * tile, -1)
    full = cols * depth
    gram = jnp.zeros((full, full), jnp.float32)
    for s in range(tile):
        rows = total[pl.ds(s, full, stride=tile), :]
        gram = gram + lax.dot_general(
            rows,
            rows,
            (((1,), (1,)), ((), ())),
            precision=lax.Precision.HIGHEST,
            preferred_element_type=jnp.float32,
        )
    gram = gram * scale
    devices = out_ref.shape[0]
    share = full // (devices // cols)
    for d in range(devices):
        x = d % cols
        start = d // cols * share
        out_ref[d, 0:share, 0:depth] = gram[start : start + share, x * depth : (x + 1) * depth]


def gram_blocks(parts, cols, rows, scale):
    _, depth, tile, r1 = parts.shape
    full = cols * depth
    return pl.pallas_call(
        functools.partial(gram_kernel, cols, scale),
        out_shape=jax.ShapeDtypeStruct((rows * cols, TILE, 128), jnp.float32),
        in_specs=[pl.BlockSpec(memory_space=pltpu.VMEM)],
        out_specs=pl.BlockSpec(memory_space=pltpu.VMEM),
        scratch_shapes=[pltpu.VMEM((full * tile, r1), jnp.float32)],
        cost_estimate=pl.CostEstimate(
            flops=2 * full * full * tile * r1, bytes_accessed=4 * parts.size, transcendentals=0
        ),
    )(parts)


def per_device(sizes, slab, factor_one, factor_two):
    zs, cols = sizes
    depth = slab.shape[0]
    r1, r2 = factor_one.shape[1], factor_two.shape[1]
    scale = 1.0 / (r1 * r2)
    own, other = project(slab, factor_one, factor_two)
    own = own + lax.ppermute(other, "core", [(0, 1), (1, 0)])
    pieces = zs * cols
    full = cols * depth
    rows = zs * CORES
    if own.shape[0] == pieces and full % rows == 0 and full // rows <= TILE and depth <= 128:
        parts = lax.all_to_all(own, ("z", "col"), 0, 0, tiled=True)
        blocks = gram_blocks(parts, cols, rows, scale)
        blocks = lax.all_to_all(blocks, ("z", "core", "col"), 0, 0, tiled=True)
        return blocks[:, : full // rows, :depth].sum(0).T
    own = own.transpose(0, 2, 1, 3).reshape(r2 // CORES, depth, r1)
    share = lax.psum_scatter(own, "z", scatter_dimension=0, tiled=True)
    whole = lax.all_gather(share, "col", axis=1, tiled=True)
    gram = jnp.einsum("skr,slr->kl", share, whole, precision=lax.Precision.HIGHEST)
    return lax.psum_scatter(gram, ("z", "core"), scatter_dimension=1, tiled=True) * scale


def solution(mesh):
    groups, rows, cols = mesh.devices.shape
    zs = rows // CORES
    fine = Mesh(mesh.devices.reshape(groups, zs, CORES, cols), ("groups", "z", "core", "col"))
    row = ("z", "core")
    return jax.shard_map(
        functools.partial(per_device, (zs, cols)),
        mesh=fine,
        in_specs=(P(("groups", "col"), row, None), P(), P(row, None)),
        out_specs=P(("groups", "col"), row),
        check_vma=False,
    )
```

```python
import functools

import jax
import jax.numpy as jnp
from jax import lax
from jax.experimental import pallas as pl
from jax.experimental.pallas import tpu as pltpu
from jax.sharding import Mesh, PartitionSpec as P

TILE = 8
CORES = 2
CHUNK = 4


def project_kernel(chunk, slab_ref, one_ref, two_ref, own_ref, other_ref, slab_buf, one_buf, two_buf, turned, sems):
    depth, width, _ = slab_ref.shape
    chunks = depth // chunk
    half = turned.shape[0] // CORES
    one_copy = pltpu.make_async_copy(one_ref, one_buf, sems.at[chunks])
    one_copy.start()
    two_copy = pltpu.make_async_copy(two_ref, two_buf, sems.at[chunks + 1])
    two_copy.start()
    copies = []
    for c in range(chunks):
        part = pl.ds(c * chunk, chunk)
        copies.append(pltpu.make_async_copy(slab_ref.at[part], slab_buf.at[part], sems.at[c]))
        copies[-1].start()
    two_copy.wait()
    turned[...] = two_buf[...].astype(jnp.float32).T
    core = lax.axis_index("core")
    two_own = turned[pl.ds(pl.multiple_of(core * half, half), half), :].astype(jnp.bfloat16)
    two_other = turned[pl.ds(pl.multiple_of((1 - core) * half, half), half), :].astype(jnp.bfloat16)
    one_copy.wait()
    for c in range(chunks):
        copies[c].wait()
        rows = slab_buf[pl.ds(c * chunk, chunk)].reshape(chunk * width, -1)
        first = jnp.dot(rows, one_buf[...], preferred_element_type=jnp.float32).astype(jnp.bfloat16)
        for q in range(chunk):
            k = c * chunk + q
            piece = first[q * width : (q + 1) * width]
            for two, out in ((two_other, other_ref), (two_own, own_ref)):
                core_part = jnp.dot(two, piece, preferred_element_type=jnp.float32)
                out[:, k] = core_part.reshape(half // TILE, TILE, -1)


def project(slab, factor_one, factor_two):
    depth, width, length = slab.shape
    r1, r2 = factor_one.shape[1], factor_two.shape[1]
    half = r2 // CORES
    chunk = CHUNK if depth % CHUNK == 0 else 1
    out = pltpu.VMEM((half // TILE, depth, TILE, r1), jnp.float32)
    return pl.pallas_call(
        functools.partial(project_kernel, chunk),
        out_shape=(out, out),
        in_specs=[
            pl.BlockSpec(memory_space=pltpu.HBM),
            pl.BlockSpec(memory_space=pltpu.HBM),
            pl.BlockSpec(memory_space=pltpu.HBM),
        ],
        out_specs=[pl.BlockSpec(memory_space=pltpu.VMEM)] * 2,
        scratch_shapes=[
            pltpu.VMEM(slab.shape, slab.dtype),
            pltpu.VMEM(factor_one.shape, factor_one.dtype),
            pltpu.VMEM(factor_two.shape, factor_two.dtype),
            pltpu.VMEM((r2, width), jnp.float32),
            pltpu.SemaphoreType.DMA((depth // chunk + 2,)),
        ],
        compiler_params=pltpu.CompilerParams(vmem_limit_bytes=32 * 2**20),
        cost_estimate=pl.CostEstimate(
            flops=2 * depth * width * r1 * (length + r2),
            bytes_accessed=2 * (slab.size + factor_one.size) + 8 * depth * half * r1,
            transcendentals=0,
        ),
    )(*(pltpu.with_memory_space_constraint(a, pltpu.HBM) for a in (slab, factor_one, factor_two)))


def gram_kernel(cols, scale, parts_ref, out_ref, total):
    sources, depth, tile, _ = parts_ref.shape
    for x in range(cols):
        value = parts_ref[x]
        for z in range(1, sources // cols):
            value = value + parts_ref[z * cols + x]
        total[pl.ds(x * depth * tile, depth * tile), :] = value.reshape(depth * tile, -1)
    full = cols * depth
    gram = jnp.zeros((full, full), jnp.float32)
    for s in range(tile):
        rows = total[pl.ds(s, full, stride=tile), :]
        gram = gram + lax.dot_general(
            rows,
            rows,
            (((1,), (1,)), ((), ())),
            precision=lax.Precision.HIGHEST,
            preferred_element_type=jnp.float32,
        )
    gram = gram * scale
    devices = out_ref.shape[0]
    share = full // (devices // cols)
    for d in range(devices):
        x = d % cols
        start = d // cols * share
        out_ref[d, 0:share, 0:depth] = gram[start : start + share, x * depth : (x + 1) * depth]


def gram_blocks(parts, cols, rows, scale):
    _, depth, tile, r1 = parts.shape
    full = cols * depth
    return pl.pallas_call(
        functools.partial(gram_kernel, cols, scale),
        out_shape=pltpu.VMEM((rows * cols, TILE, 128), jnp.float32),
        in_specs=[pl.BlockSpec(memory_space=pltpu.VMEM)],
        out_specs=pl.BlockSpec(memory_space=pltpu.VMEM),
        scratch_shapes=[pltpu.VMEM((full * tile, r1), jnp.float32)],
        cost_estimate=pl.CostEstimate(
            flops=2 * full * full * tile * r1, bytes_accessed=4 * parts.size, transcendentals=0
        ),
    )(parts)


def per_device(sizes, slab, factor_one, factor_two):
    zs, cols = sizes
    depth = slab.shape[0]
    r1, r2 = factor_one.shape[1], factor_two.shape[1]
    scale = 1.0 / (r1 * r2)
    own, other = project(slab, factor_one, factor_two)
    own = own + lax.ppermute(other, "core", [(0, 1), (1, 0)])
    pieces = zs * cols
    full = cols * depth
    rows = zs * CORES
    if own.shape[0] == pieces and full % rows == 0 and full // rows <= TILE and depth <= 128:
        parts = lax.all_to_all(own, ("z", "col"), 0, 0, tiled=True)
        blocks = gram_blocks(parts, cols, rows, scale)
        blocks = lax.all_to_all(blocks, ("z", "core", "col"), 0, 0, tiled=True)
        return blocks[:, : full // rows, :depth].sum(0).T
    own = own.transpose(0, 2, 1, 3).reshape(r2 // CORES, depth, r1)
    share = lax.psum_scatter(own, "z", scatter_dimension=0, tiled=True)
    whole = lax.all_gather(share, "col", axis=1, tiled=True)
    gram = jnp.einsum("skr,slr->kl", share, whole, precision=lax.Precision.HIGHEST)
    return lax.psum_scatter(gram, ("z", "core"), scatter_dimension=1, tiled=True) * scale


def solution(mesh):
    groups, rows, cols = mesh.devices.shape
    zs = rows // CORES
    fine = Mesh(mesh.devices.reshape(groups, zs, CORES, cols), ("groups", "z", "core", "col"))
    row = ("z", "core")
    return jax.shard_map(
        functools.partial(per_device, (zs, cols)),
        mesh=fine,
        in_specs=(P(("groups", "col"), row, None), P(), P(row, None)),
        out_specs=P(("groups", "col"), row),
        check_vma=False,
    )
```

```python
import functools

import jax
import jax.numpy as jnp
from jax import lax
from jax.experimental import pallas as pl
from jax.experimental.pallas import tpu as pltpu
from jax.sharding import Mesh, PartitionSpec as P

TILE = 8
CORES = 2
CHUNK = 4
RING = 4
FIRST = 1
SECOND = 3


def project_kernel(chunk, starts, slab_ref, one_ref, two_ref, *rest):
    outs, (slab_buf, one_buf, two_buf, turned, sems) = rest[:-5], rest[-5:]
    depth, width, _ = slab_ref.shape
    chunks = depth // chunk
    one_copy = pltpu.make_async_copy(one_ref, one_buf, sems.at[chunks])
    one_copy.start()
    two_copy = pltpu.make_async_copy(two_ref, two_buf, sems.at[chunks + 1])
    two_copy.start()
    copies = []
    for c in range(chunks):
        part = pl.ds(c * chunk, chunk)
        copies.append(pltpu.make_async_copy(slab_ref.at[part], slab_buf.at[part], sems.at[c]))
        copies[-1].start()
    two_copy.wait()
    turned[...] = two_buf[...].astype(jnp.float32).T
    pieces = [turned[pl.ds(pl.multiple_of(s, TILE), TILE), :] for s in starts()]
    two = jnp.concatenate(pieces, axis=0).astype(jnp.bfloat16)
    share = two.shape[0] // len(outs)

    def second(c, first):
        for q in range(chunk):
            core_part = jnp.dot(two, first[q * width : (q + 1) * width], preferred_element_type=jnp.float32)
            for o, out in enumerate(outs):
                piece = core_part[o * share : (o + 1) * share]
                out[:, c * chunk + q] = piece.reshape(share // TILE, TILE, -1)

    one_copy.wait()
    late = None
    for c in range(chunks):
        copies[c].wait()
        rows = slab_buf[pl.ds(c * chunk, chunk)].reshape(chunk * width, -1)
        first = jnp.dot(rows, one_buf[...], preferred_element_type=jnp.float32).astype(jnp.bfloat16)
        if late is not None:
            second(c - 1, late)
        late = first
    second(chunks - 1, late)


def project(slab, factor_one, factor_two, starts, outputs):
    depth, width, length = slab.shape
    r1, r2 = factor_one.shape[1], factor_two.shape[1]
    chunk = CHUNK if depth % CHUNK == 0 else 1
    out = pltpu.VMEM((r2 // TILE // outputs, depth, TILE, r1), jnp.float32)
    return pl.pallas_call(
        functools.partial(project_kernel, chunk, starts),
        out_shape=(out,) * outputs,
        in_specs=[pl.BlockSpec(memory_space=pltpu.HBM)] * 3,
        out_specs=[pl.BlockSpec(memory_space=pltpu.VMEM)] * outputs,
        scratch_shapes=[
            pltpu.VMEM(slab.shape, slab.dtype),
            pltpu.VMEM(factor_one.shape, factor_one.dtype),
            pltpu.VMEM(factor_two.shape, factor_two.dtype),
            pltpu.VMEM((r2, width), jnp.float32),
            pltpu.SemaphoreType.DMA((depth // chunk + 2,)),
        ],
        compiler_params=pltpu.CompilerParams(vmem_limit_bytes=32 * 2**20),
        cost_estimate=pl.CostEstimate(
            flops=2 * depth * width * r1 * (length + r2),
            bytes_accessed=2 * (slab.size + factor_one.size) + 4 * depth * r2 * r1,
            transcendentals=0,
        ),
    )(*(pltpu.with_memory_space_constraint(a, pltpu.HBM) for a in (slab, factor_one, factor_two)))


def gram_kernel(scale, own_ref, far_ref, out_ref, flag_ref, total, gram):
    groups, depth, tile, _ = own_ref.shape
    z, core, x = (lax.axis_index(name) for name in ("z", "core", "col"))
    chips, share, _ = out_ref.shape
    size = depth * tile
    value = jnp.zeros((2 * depth, depth), jnp.float32)
    for g in range(groups):
        total[g, pl.ds(pl.multiple_of(x * size, size), size), :] = own_ref[g].reshape(size, -1)
        total[g, pl.ds(pl.multiple_of((1 - x) * size, size), size), :] = far_ref[g].reshape(size, -1)
    for g in range(groups):
        for s in range(tile):
            rows = total[g, pl.ds(s, 2 * depth, stride=tile), :]
            own = total[g, pl.ds(x * size + s, depth, stride=tile), :]
            value = value + lax.dot_general(
                rows,
                own,
                (((1,), (1,)), ((), ())),
                precision=lax.Precision.HIGHEST,
                preferred_element_type=jnp.float32,
            )
    gram[:, 0:depth] = value * scale
    for slot, hops in enumerate(((), (SECOND,), (FIRST,), (FIRST, SECOND))):
        to_z = z
        for hop in hops:
            to_z = jnp.bitwise_xor(to_z, hop)
        out_ref[slot] = gram[pl.ds(pl.multiple_of(to_z * share, TILE), share), :]
    flag_ref[...] = jnp.full(flag_ref.shape, core, jnp.int32)


def gram_blocks(own, far, chips, scale):
    groups, depth, tile, r1 = own.shape
    full = 2 * depth
    return pl.pallas_call(
        functools.partial(gram_kernel, scale),
        out_shape=(pltpu.VMEM((chips, full // chips, 128), jnp.float32), pltpu.VMEM((TILE, 128), jnp.int32)),
        in_specs=[pl.BlockSpec(memory_space=pltpu.VMEM)] * 2,
        out_specs=[pl.BlockSpec(memory_space=pltpu.VMEM)] * 2,
        scratch_shapes=[
            pltpu.VMEM((groups, full * tile, r1), jnp.float32),
            pltpu.VMEM((full, 128), jnp.float32),
        ],
        cost_estimate=pl.CostEstimate(
            flops=2 * groups * full * depth * tile * r1, bytes_accessed=8 * own.size, transcendentals=0
        ),
    )(*(pltpu.with_memory_space_constraint(a, pltpu.VMEM) for a in (own, far)))


def send(value, zs, step, cross=0):
    pairs = [(z * CORES + core, step(z) * CORES + (core ^ cross)) for z in range(zs) for core in range(CORES)]
    return lax.ppermute(value, ("z", "core"), pairs)


def swap(value, axis):
    return lax.ppermute(value, axis, [(0, 1), (1, 0)])


RING_STEPS = (2, 1, -1, 0)


def ring_starts(zs, half, width):
    z, core = lax.axis_index("z"), lax.axis_index("core")
    starts = []
    for side in (1 - core, core):
        for step in RING_STEPS:
            to_z = lax.rem(z + step + zs, zs)
            starts += [side * half + to_z * width + s for s in range(0, width, TILE)]
    return starts


def ring_plan(zs, scale, slab, factor_one, factor_two):
    half = factor_two.shape[1] // CORES
    starts = functools.partial(ring_starts, zs, half, half // zs)
    parts = project(slab, factor_one, factor_two, starts, 2 * zs)
    others, owns = parts[:zs], parts[zs:]
    swapped = [swap(other, "core") for other in others]
    chip = [own + got for own, got in zip(owns, swapped)]
    got = [send(value, zs, lambda z, step=step: (z + step) % zs) for value, step in zip(chip[:-1], RING_STEPS)]
    own = chip[-1] + got[0] + got[1] + got[2]
    blocks, flag = gram_blocks(own, swap(own, "col"), zs, scale)
    blocks = blocks + swap(blocks, "core")
    pair = blocks[:2] + send(blocks[2:], zs, lambda z: z ^ FIRST, cross=1)
    last = pair[0] + send(pair[1], zs, lambda z: z ^ SECOND, cross=1)
    depth, rows = slab.shape[0], last.shape[0] // CORES
    return jnp.where(flag[:rows, :depth] == 1, last[rows:, :depth], last[:rows, :depth]).T


def general_plan(scale, slab, factor_one, factor_two):
    depth = slab.shape[0]
    r1, r2 = factor_one.shape[1], factor_two.shape[1]
    half = r2 // CORES

    def starts():
        core = lax.axis_index("core")
        return [side * half + s for side in (1 - core, core) for s in range(0, half, TILE)]

    other, own = project(slab, factor_one, factor_two, starts, 2)
    own = own + swap(other, "core")
    own = own.transpose(0, 2, 1, 3).reshape(half, depth, r1)
    share = lax.psum_scatter(own, "z", scatter_dimension=0, tiled=True)
    whole = lax.all_gather(share, "col", axis=1, tiled=True)
    gram = jnp.einsum("skr,slr->kl", share, whole, precision=lax.Precision.HIGHEST)
    return lax.psum_scatter(gram, ("z", "core"), scatter_dimension=1, tiled=True) * scale


def per_device(zs, cols, slab, factor_one, factor_two):
    r1, r2 = factor_one.shape[1], factor_two.shape[1]
    scale = 1.0 / (r1 * r2)
    depth = slab.shape[0]
    if zs == RING and cols == 2 and r2 % (CORES * zs * TILE) == 0 and cols * depth == zs * TILE:
        return ring_plan(zs, scale, slab, factor_one, factor_two)
    return general_plan(scale, slab, factor_one, factor_two)


def solution(mesh):
    groups, rows, cols = mesh.devices.shape
    zs = rows // CORES
    fine = Mesh(mesh.devices.reshape(groups, zs, CORES, cols), ("groups", "z", "core", "col"))
    row = ("z", "core")
    return jax.shard_map(
        functools.partial(per_device, zs, cols),
        mesh=fine,
        in_specs=(P(("groups", "col"), row, None), P(), P(row, None)),
        out_specs=P(("groups", "col"), row),
        check_vma=False,
    )
```

```python
import functools

import jax
import jax.numpy as jnp
from jax import lax
from jax.experimental import pallas as pl
from jax.experimental.pallas import tpu as pltpu
from jax.sharding import Mesh, PartitionSpec as P

TILE = 8
CORES = 2
CHUNK = 4
RING = 4
FIRST = 1
SECOND = 2


def project_kernel(chunk, starts, slab_ref, one_ref, two_ref, *rest):
    outs, (slab_buf, one_buf, two_buf, turned, sems) = rest[:-5], rest[-5:]
    depth, width, _ = slab_ref.shape
    chunks = depth // chunk
    one_copy = pltpu.make_async_copy(one_ref, one_buf, sems.at[chunks])
    one_copy.start()
    two_copy = pltpu.make_async_copy(two_ref, two_buf, sems.at[chunks + 1])
    two_copy.start()
    copies = []
    for c in range(chunks):
        part = pl.ds(c * chunk, chunk)
        copies.append(pltpu.make_async_copy(slab_ref.at[part], slab_buf.at[part], sems.at[c]))
        copies[-1].start()
    two_copy.wait()
    turned[...] = two_buf[...].astype(jnp.float32).T
    pieces = [turned[pl.ds(pl.multiple_of(s, TILE), TILE), :] for s in starts()]
    two = jnp.concatenate(pieces, axis=0).astype(jnp.bfloat16)
    share = two.shape[0] // len(outs)

    def second(c, first):
        for q in range(chunk):
            core_part = jnp.dot(two, first[q * width : (q + 1) * width], preferred_element_type=jnp.float32)
            for o, out in enumerate(outs):
                piece = core_part[o * share : (o + 1) * share]
                out[:, c * chunk + q] = piece.reshape(share // TILE, TILE, -1)

    one_copy.wait()
    late = None
    for c in range(chunks):
        copies[c].wait()
        rows = slab_buf[pl.ds(c * chunk, chunk)].reshape(chunk * width, -1)
        first = jnp.dot(rows, one_buf[...], preferred_element_type=jnp.float32).astype(jnp.bfloat16)
        if late is not None:
            second(c - 1, late)
        late = first
    second(chunks - 1, late)


def project(slab, factor_one, factor_two, starts, outputs):
    depth, width, length = slab.shape
    r1, r2 = factor_one.shape[1], factor_two.shape[1]
    chunk = CHUNK if depth % CHUNK == 0 else 1
    out = pltpu.VMEM((r2 // TILE // outputs, depth, TILE, r1), jnp.float32)
    return pl.pallas_call(
        functools.partial(project_kernel, chunk, starts),
        out_shape=(out,) * outputs,
        in_specs=[pl.BlockSpec(memory_space=pltpu.HBM)] * 3,
        out_specs=[pl.BlockSpec(memory_space=pltpu.VMEM)] * outputs,
        scratch_shapes=[
            pltpu.VMEM(slab.shape, slab.dtype),
            pltpu.VMEM(factor_one.shape, factor_one.dtype),
            pltpu.VMEM(factor_two.shape, factor_two.dtype),
            pltpu.VMEM((r2, width), jnp.float32),
            pltpu.SemaphoreType.DMA((depth // chunk + 2,)),
        ],
        compiler_params=pltpu.CompilerParams(vmem_limit_bytes=32 * 2**20),
        cost_estimate=pl.CostEstimate(
            flops=2 * depth * width * r1 * (length + r2),
            bytes_accessed=2 * (slab.size + factor_one.size) + 4 * depth * r2 * r1,
            transcendentals=0,
        ),
    )(*(pltpu.with_memory_space_constraint(a, pltpu.HBM) for a in (slab, factor_one, factor_two)))


def gram_kernel(scale, own_ref, far_ref, out_ref, flag_ref, total, gram):
    groups, depth, tile, _ = own_ref.shape
    z, core, x = (lax.axis_index(name) for name in ("z", "core", "col"))
    chips, share, _ = out_ref.shape
    size = depth * tile
    value = jnp.zeros((2 * depth, depth), jnp.float32)
    for g in range(groups):
        total[g, pl.ds(pl.multiple_of(x * size, size), size), :] = own_ref[g].reshape(size, -1)
        total[g, pl.ds(pl.multiple_of((1 - x) * size, size), size), :] = far_ref[g].reshape(size, -1)
    for g in range(groups):
        for s in range(tile):
            rows = total[g, pl.ds(s, 2 * depth, stride=tile), :]
            own = total[g, pl.ds(x * size + s, depth, stride=tile), :]
            value = value + lax.dot_general(
                rows,
                own,
                (((1,), (1,)), ((), ())),
                precision=lax.Precision.HIGHEST,
                preferred_element_type=jnp.float32,
            )
    gram[:, 0:depth] = value * scale
    for slot, hops in enumerate(((), (SECOND,), (FIRST,), (FIRST, SECOND))):
        to_z = z
        for hop in hops:
            to_z = jnp.bitwise_xor(to_z, hop)
        out_ref[slot] = gram[pl.ds(pl.multiple_of(to_z * share, TILE), share), :]
    flag_ref[...] = jnp.full(flag_ref.shape, core, jnp.int32)


def gram_blocks(own, far, chips, scale):
    groups, depth, tile, r1 = own.shape
    full = 2 * depth
    return pl.pallas_call(
        functools.partial(gram_kernel, scale),
        out_shape=(pltpu.VMEM((chips, full // chips, 128), jnp.float32), pltpu.VMEM((TILE, 128), jnp.int32)),
        in_specs=[pl.BlockSpec(memory_space=pltpu.VMEM)] * 2,
        out_specs=[pl.BlockSpec(memory_space=pltpu.VMEM)] * 2,
        scratch_shapes=[
            pltpu.VMEM((groups, full * tile, r1), jnp.float32),
            pltpu.VMEM((full, 128), jnp.float32),
        ],
        cost_estimate=pl.CostEstimate(
            flops=2 * groups * full * depth * tile * r1, bytes_accessed=8 * own.size, transcendentals=0
        ),
    )(*(pltpu.with_memory_space_constraint(a, pltpu.VMEM) for a in (own, far)))


def hop(value, zs, masks, cross=0):
    pairs = [
        (z * CORES + core, (z ^ masks[core]) * CORES + (core ^ cross)) for z in range(zs) for core in range(CORES)
    ]
    return lax.ppermute(value, ("z", "core"), pairs)


def swap(value, axis):
    return lax.ppermute(value, axis, [(0, 1), (1, 0)])


FIRST_HOP = (FIRST, SECOND)
SECOND_HOP = (SECOND, FIRST)


def ring_starts(half, width):
    z, core = lax.axis_index("z"), lax.axis_index("core")
    starts = []
    for to_core in (1 - core, core):
        one, two = (to_core * (hops[1] - hops[0]) + hops[0] for hops in (FIRST_HOP, SECOND_HOP))
        for mask in (FIRST ^ SECOND, one, two, 0):
            starts += [to_core * half + jnp.bitwise_xor(z, mask) * width + s for s in range(0, width, TILE)]
    return starts


def ring_plan(zs, scale, slab, factor_one, factor_two):
    half = factor_two.shape[1] // CORES
    starts = functools.partial(ring_starts, half, half // zs)
    parts = project(slab, factor_one, factor_two, starts, 2 * zs)
    passed, given, across, own = (o + swap(t, "core") for t, o in zip(parts[:zs], parts[zs:]))
    arrived = hop(passed, zs, FIRST_HOP)
    beside = hop(given, zs, FIRST_HOP)
    own = own + beside + hop(across + arrived, zs, SECOND_HOP)
    blocks, flag = gram_blocks(own, swap(own, "col"), zs, scale)
    blocks = blocks + swap(blocks, "core")
    pair = blocks[:2] + hop(blocks[2:], zs, (FIRST, FIRST), cross=1)
    last = pair[0] + hop(pair[1], zs, (SECOND, SECOND), cross=1)
    depth, rows = slab.shape[0], last.shape[0] // CORES
    return jnp.where(flag[:rows, :depth] == 1, last[rows:, :depth], last[:rows, :depth]).T


def general_plan(scale, slab, factor_one, factor_two):
    depth = slab.shape[0]
    r1, r2 = factor_one.shape[1], factor_two.shape[1]
    half = r2 // CORES

    def starts():
        core = lax.axis_index("core")
        return [side * half + s for side in (1 - core, core) for s in range(0, half, TILE)]

    other, own = project(slab, factor_one, factor_two, starts, 2)
    own = own + swap(other, "core")
    own = own.transpose(0, 2, 1, 3).reshape(half, depth, r1)
    share = lax.psum_scatter(own, "z", scatter_dimension=0, tiled=True)
    whole = lax.all_gather(share, "col", axis=1, tiled=True)
    gram = jnp.einsum("skr,slr->kl", share, whole, precision=lax.Precision.HIGHEST)
    return lax.psum_scatter(gram, ("z", "core"), scatter_dimension=1, tiled=True) * scale


def per_device(zs, cols, slab, factor_one, factor_two):
    r1, r2 = factor_one.shape[1], factor_two.shape[1]
    scale = 1.0 / (r1 * r2)
    depth = slab.shape[0]
    if zs == RING and cols == 2 and r2 % (CORES * zs * TILE) == 0 and cols * depth == zs * TILE:
        return ring_plan(zs, scale, slab, factor_one, factor_two)
    return general_plan(scale, slab, factor_one, factor_two)


def solution(mesh):
    groups, rows, cols = mesh.devices.shape
    zs = rows // CORES
    fine = Mesh(mesh.devices.reshape(groups, zs, CORES, cols), ("groups", "z", "core", "col"))
    row = ("z", "core")
    return jax.shard_map(
        functools.partial(per_device, zs, cols),
        mesh=fine,
        in_specs=(P(("groups", "col"), row, None), P(), P(row, None)),
        out_specs=P(("groups", "col"), row),
        check_vma=False,
    )
```

```python
import functools

import jax
import jax.numpy as jnp
from jax import lax
from jax.experimental import pallas as pl
from jax.experimental.pallas import tpu as pltpu
from jax.sharding import Mesh, PartitionSpec as P

TILE = 8
CORES = 2
CHUNK = 4
RING = 4
FIRST = 1
SECOND = 2


def project_kernel(chunk, starts, slab_ref, one_ref, two_ref, *rest):
    outs, (slab_buf, one_buf, two_buf, turned, sems) = rest[:-5], rest[-5:]
    depth, width, _ = slab_ref.shape
    chunks = depth // chunk
    one_copy = pltpu.make_async_copy(one_ref, one_buf, sems.at[chunks])
    one_copy.start()
    two_copy = pltpu.make_async_copy(two_ref, two_buf, sems.at[chunks + 1])
    two_copy.start()
    copies = []
    for c in range(chunks):
        part = pl.ds(c * chunk, chunk)
        copies.append(pltpu.make_async_copy(slab_ref.at[part], slab_buf.at[part], sems.at[c]))
        copies[-1].start()
    two_copy.wait()
    turned[...] = two_buf[...].astype(jnp.float32).T
    pieces = [turned[pl.ds(pl.multiple_of(s, TILE), TILE), :] for s in starts()]
    two = jnp.concatenate(pieces, axis=0).astype(jnp.bfloat16)
    share = two.shape[0] // len(outs)

    def second(c, first):
        for q in range(chunk):
            core_part = jnp.dot(two, first[q * width : (q + 1) * width], preferred_element_type=jnp.float32)
            for o, out in enumerate(outs):
                piece = core_part[o * share : (o + 1) * share]
                out[:, c * chunk + q] = piece.reshape(share // TILE, TILE, -1)

    one_copy.wait()
    late = None
    for c in range(chunks):
        copies[c].wait()
        rows = slab_buf[pl.ds(c * chunk, chunk)].reshape(chunk * width, -1)
        first = jnp.dot(rows, one_buf[...], preferred_element_type=jnp.float32).astype(jnp.bfloat16)
        if late is not None:
            second(c - 1, late)
        late = first
    second(chunks - 1, late)


def project(slab, factor_one, factor_two, starts, outputs):
    depth, width, length = slab.shape
    r1, r2 = factor_one.shape[1], factor_two.shape[1]
    chunk = CHUNK if depth % CHUNK == 0 else 1
    out = pltpu.VMEM((r2 // TILE // outputs, depth, TILE, r1), jnp.float32)
    return pl.pallas_call(
        functools.partial(project_kernel, chunk, starts),
        out_shape=(out,) * outputs,
        in_specs=[pl.BlockSpec(memory_space=pltpu.HBM)] * 3,
        out_specs=[pl.BlockSpec(memory_space=pltpu.VMEM)] * outputs,
        scratch_shapes=[
            pltpu.VMEM(slab.shape, slab.dtype),
            pltpu.VMEM(factor_one.shape, factor_one.dtype),
            pltpu.VMEM(factor_two.shape, factor_two.dtype),
            pltpu.VMEM((r2, width), jnp.float32),
            pltpu.SemaphoreType.DMA((depth // chunk + 2,)),
        ],
        compiler_params=pltpu.CompilerParams(vmem_limit_bytes=32 * 2**20),
        cost_estimate=pl.CostEstimate(
            flops=2 * depth * width * r1 * (length + r2),
            bytes_accessed=2 * (slab.size + factor_one.size) + 4 * depth * r2 * r1,
            transcendentals=0,
        ),
    )(*(pltpu.with_memory_space_constraint(a, pltpu.HBM) for a in (slab, factor_one, factor_two)))


def gram_kernel(scale, own_ref, own_add, far_ref, far_add, out_ref, flag_ref, total, gram):
    groups, depth, tile, _ = own_ref.shape
    z, core, x = (lax.axis_index(name) for name in ("z", "core", "col"))
    chips, share, _ = out_ref.shape
    size = depth * tile
    value = jnp.zeros((2 * depth, depth), jnp.float32)
    for g in range(groups):
        total[g, pl.ds(pl.multiple_of(x * size, size), size), :] = (own_ref[g] + own_add[g]).reshape(size, -1)
        total[g, pl.ds(pl.multiple_of((1 - x) * size, size), size), :] = (far_ref[g] + far_add[g]).reshape(size, -1)
    for g in range(groups):
        for s in range(tile):
            rows = total[g, pl.ds(s, 2 * depth, stride=tile), :]
            own = total[g, pl.ds(x * size + s, depth, stride=tile), :]
            value = value + lax.dot_general(
                rows,
                own,
                (((1,), (1,)), ((), ())),
                precision=lax.Precision.HIGHEST,
                preferred_element_type=jnp.float32,
            )
    gram[:, 0:depth] = value * scale
    for slot, hops in enumerate(((), (SECOND,), (FIRST,), (FIRST, SECOND))):
        to_z = z
        for hop in hops:
            to_z = jnp.bitwise_xor(to_z, hop)
        out_ref[slot] = gram[pl.ds(pl.multiple_of(to_z * share, TILE), share), :]
    flag_ref[...] = jnp.full(flag_ref.shape, core, jnp.int32)


def gram_blocks(own, far, chips, scale):
    groups, depth, tile, r1 = own[0].shape
    full = 2 * depth
    return pl.pallas_call(
        functools.partial(gram_kernel, scale),
        out_shape=(pltpu.VMEM((chips, full // chips, 128), jnp.float32), pltpu.VMEM((TILE, 128), jnp.int32)),
        in_specs=[pl.BlockSpec(memory_space=pltpu.VMEM)] * 4,
        out_specs=[pl.BlockSpec(memory_space=pltpu.VMEM)] * 2,
        scratch_shapes=[
            pltpu.VMEM((groups, full * tile, r1), jnp.float32),
            pltpu.VMEM((full, 128), jnp.float32),
        ],
        cost_estimate=pl.CostEstimate(
            flops=2 * groups * full * depth * tile * r1, bytes_accessed=16 * own[0].size, transcendentals=0
        ),
    )(*(pltpu.with_memory_space_constraint(a, pltpu.VMEM) for a in own + far))


def hop(value, zs, masks, cross=0, flip=0):
    pairs = []
    for z in range(zs):
        for core in range(CORES):
            for x in range(2):
                to = ((z ^ masks[core]) * CORES + (core ^ cross)) * 2 + (x ^ flip)
                pairs.append(((z * CORES + core) * 2 + x, to))
    return lax.ppermute(value, ("z", "core", "col"), pairs)


def swap(value, axis):
    return lax.ppermute(value, axis, [(0, 1), (1, 0)])


FIRST_HOP = (FIRST, SECOND)
SECOND_HOP = (SECOND, FIRST)


def ring_starts(half, width):
    z, core = lax.axis_index("z"), lax.axis_index("core")
    starts = []
    for to_core in (1 - core, core):
        one, two = (to_core * (hops[1] - hops[0]) + hops[0] for hops in (FIRST_HOP, SECOND_HOP))
        for mask in (FIRST ^ SECOND, one, two, 0):
            starts += [to_core * half + jnp.bitwise_xor(z, mask) * width + s for s in range(0, width, TILE)]
    return starts


def ring_plan(zs, scale, slab, factor_one, factor_two):
    half = factor_two.shape[1] // CORES
    starts = functools.partial(ring_starts, half, half // zs)
    parts = project(slab, factor_one, factor_two, starts, 2 * zs)
    passed, given, across, own = (o + swap(t, "core") for t, o in zip(parts[:zs], parts[zs:]))
    arrived = hop(passed, zs, FIRST_HOP)
    beside = hop(given, zs, FIRST_HOP)
    onward = across + arrived
    far_add = hop(onward, zs, SECOND_HOP, flip=1)
    own_add = hop(onward, zs, SECOND_HOP)
    own = lax.optimization_barrier((own, onward))[0] + beside
    blocks, flag = gram_blocks((own, own_add), (swap(own, "col"), far_add), zs, scale)
    blocks = blocks + swap(blocks, "core")
    pair = blocks[:2] + hop(blocks[2:], zs, (FIRST, FIRST), cross=1)
    last = pair[0] + hop(pair[1], zs, (SECOND, SECOND), cross=1)
    depth, rows = slab.shape[0], last.shape[0] // CORES
    return jnp.where(flag[:rows, :depth] == 1, last[rows:, :depth], last[:rows, :depth]).T


def general_plan(scale, slab, factor_one, factor_two):
    depth = slab.shape[0]
    r1, r2 = factor_one.shape[1], factor_two.shape[1]
    half = r2 // CORES

    def starts():
        core = lax.axis_index("core")
        return [side * half + s for side in (1 - core, core) for s in range(0, half, TILE)]

    other, own = project(slab, factor_one, factor_two, starts, 2)
    own = own + swap(other, "core")
    own = own.transpose(0, 2, 1, 3).reshape(half, depth, r1)
    share = lax.psum_scatter(own, "z", scatter_dimension=0, tiled=True)
    whole = lax.all_gather(share, "col", axis=1, tiled=True)
    gram = jnp.einsum("skr,slr->kl", share, whole, precision=lax.Precision.HIGHEST)
    return lax.psum_scatter(gram, ("z", "core"), scatter_dimension=1, tiled=True) * scale


def per_device(zs, cols, slab, factor_one, factor_two):
    r1, r2 = factor_one.shape[1], factor_two.shape[1]
    scale = 1.0 / (r1 * r2)
    depth = slab.shape[0]
    if zs == RING and cols == 2 and r2 % (CORES * zs * TILE) == 0 and cols * depth == zs * TILE:
        return ring_plan(zs, scale, slab, factor_one, factor_two)
    return general_plan(scale, slab, factor_one, factor_two)


def solution(mesh):
    groups, rows, cols = mesh.devices.shape
    zs = rows // CORES
    fine = Mesh(mesh.devices.reshape(groups, zs, CORES, cols), ("groups", "z", "core", "col"))
    row = ("z", "core")
    return jax.shard_map(
        functools.partial(per_device, zs, cols),
        mesh=fine,
        in_specs=(P(("groups", "col"), row, None), P(), P(row, None)),
        out_specs=P(("groups", "col"), row),
        check_vma=False,
    )
```

```python
import functools

import jax
import jax.numpy as jnp
from jax import lax
from jax.experimental import pallas as pl
from jax.experimental.pallas import tpu as pltpu
from jax.sharding import Mesh, PartitionSpec as P

TILE = 8
CORES = 2
CHUNK = 4
RING = 4
FIRST = 1
SECOND = 2


def project_kernel(chunk, starts, slab_ref, one_ref, two_ref, *rest):
    outs, (slab_buf, one_buf, two_buf, turned, sems) = rest[:-5], rest[-5:]
    depth, width, _ = slab_ref.shape
    chunks = depth // chunk
    copies = []
    for c in range(chunks):
        part = pl.ds(c * chunk, chunk)
        copies.append(pltpu.make_async_copy(slab_ref.at[part], slab_buf.at[part], sems.at[c]))
    copies[0].start()
    one_copy = pltpu.make_async_copy(one_ref, one_buf, sems.at[chunks])
    one_copy.start()
    two_copy = pltpu.make_async_copy(two_ref, two_buf, sems.at[chunks + 1])
    two_copy.start()
    for copy in copies[1:]:
        copy.start()
    two_copy.wait()
    turned[...] = two_buf[...].astype(jnp.float32).T
    pieces = [turned[pl.ds(pl.multiple_of(s, TILE), TILE), :] for s in starts()]
    two = jnp.concatenate(pieces, axis=0).astype(jnp.bfloat16)
    share = two.shape[0] // len(outs)

    def second(c, first):
        for q in range(chunk):
            core_part = jnp.dot(two, first[q * width : (q + 1) * width], preferred_element_type=jnp.float32)
            for o, out in enumerate(outs):
                piece = core_part[o * share : (o + 1) * share]
                out[:, c * chunk + q] = piece.reshape(share // TILE, TILE, -1)

    one_copy.wait()
    late = None
    for c in range(chunks):
        copies[c].wait()
        rows = slab_buf[pl.ds(c * chunk, chunk)].reshape(chunk * width, -1)
        middle = rows.shape[1] // 2
        first = jnp.dot(rows[:, :middle], one_buf[:middle], preferred_element_type=jnp.float32)
        first = first + jnp.dot(rows[:, middle:], one_buf[middle:], preferred_element_type=jnp.float32)
        first = first.astype(jnp.bfloat16)
        if late is not None:
            second(c - 1, late)
        late = first
    second(chunks - 1, late)


def project(slab, factor_one, factor_two, starts, outputs):
    depth, width, length = slab.shape
    r1, r2 = factor_one.shape[1], factor_two.shape[1]
    chunk = CHUNK if depth % CHUNK == 0 else 1
    out = pltpu.VMEM((r2 // TILE // outputs, depth, TILE, r1), jnp.float32)
    return pl.pallas_call(
        functools.partial(project_kernel, chunk, starts),
        out_shape=(out,) * outputs,
        in_specs=[pl.BlockSpec(memory_space=pltpu.HBM)] * 3,
        out_specs=[pl.BlockSpec(memory_space=pltpu.VMEM)] * outputs,
        scratch_shapes=[
            pltpu.VMEM(slab.shape, slab.dtype),
            pltpu.VMEM(factor_one.shape, factor_one.dtype),
            pltpu.VMEM(factor_two.shape, factor_two.dtype),
            pltpu.VMEM((r2, width), jnp.float32),
            pltpu.SemaphoreType.DMA((depth // chunk + 2,)),
        ],
        compiler_params=pltpu.CompilerParams(vmem_limit_bytes=32 * 2**20),
        cost_estimate=pl.CostEstimate(
            flops=2 * depth * width * r1 * (length + r2),
            bytes_accessed=2 * (slab.size + factor_one.size) + 4 * depth * r2 * r1,
            transcendentals=0,
        ),
    )(*(pltpu.with_memory_space_constraint(a, pltpu.HBM) for a in (slab, factor_one, factor_two)))


def gram_kernel(scale, own_ref, own_add, far_ref, far_add, out_ref, flag_ref, total, gram):
    groups, depth, tile, _ = own_ref.shape
    z, core, x = (lax.axis_index(name) for name in ("z", "core", "col"))
    chips, share, _ = out_ref.shape
    size = depth * tile
    value = jnp.zeros((2 * depth, depth), jnp.float32)
    for g in range(groups):
        total[g, pl.ds(pl.multiple_of(x * size, size), size), :] = (own_ref[g] + own_add[g]).reshape(size, -1)
        total[g, pl.ds(pl.multiple_of((1 - x) * size, size), size), :] = (far_ref[g] + far_add[g]).reshape(size, -1)
    for g in range(groups):
        for s in range(tile):
            rows = total[g, pl.ds(s, 2 * depth, stride=tile), :]
            own = total[g, pl.ds(x * size + s, depth, stride=tile), :]
            value = value + lax.dot_general(
                rows,
                own,
                (((1,), (1,)), ((), ())),
                precision=lax.Precision.HIGHEST,
                preferred_element_type=jnp.float32,
            )
    gram[:, 0:depth] = value * scale
    for slot, hops in enumerate(((), (SECOND,), (FIRST,), (FIRST, SECOND))):
        to_z = z
        for hop in hops:
            to_z = jnp.bitwise_xor(to_z, hop)
        out_ref[slot] = gram[pl.ds(pl.multiple_of(to_z * share, TILE), share), :]
    flag_ref[...] = jnp.full(flag_ref.shape, core, jnp.int32)


def gram_blocks(own, far, chips, scale):
    groups, depth, tile, r1 = own[0].shape
    full = 2 * depth
    return pl.pallas_call(
        functools.partial(gram_kernel, scale),
        out_shape=(pltpu.VMEM((chips, full // chips, 128), jnp.float32), pltpu.VMEM((TILE, 128), jnp.int32)),
        in_specs=[pl.BlockSpec(memory_space=pltpu.VMEM)] * 4,
        out_specs=[pl.BlockSpec(memory_space=pltpu.VMEM)] * 2,
        scratch_shapes=[
            pltpu.VMEM((groups, full * tile, r1), jnp.float32),
            pltpu.VMEM((full, 128), jnp.float32),
        ],
        cost_estimate=pl.CostEstimate(
            flops=2 * groups * full * depth * tile * r1, bytes_accessed=16 * own[0].size, transcendentals=0
        ),
    )(*(pltpu.with_memory_space_constraint(a, pltpu.VMEM) for a in own + far))


def hop(value, zs, masks, cross=0, flip=0):
    pairs = []
    for z in range(zs):
        for core in range(CORES):
            for x in range(2):
                to = ((z ^ masks[core]) * CORES + (core ^ cross)) * 2 + (x ^ flip)
                pairs.append(((z * CORES + core) * 2 + x, to))
    return lax.ppermute(value, ("z", "core", "col"), pairs)


def swap(value, axis):
    return lax.ppermute(value, axis, [(0, 1), (1, 0)])


FIRST_HOP = (FIRST, SECOND)
SECOND_HOP = (SECOND, FIRST)


def ring_starts(half, width):
    z, core = lax.axis_index("z"), lax.axis_index("core")
    starts = []
    for to_core in (1 - core, core):
        one, two = (to_core * (hops[1] - hops[0]) + hops[0] for hops in (FIRST_HOP, SECOND_HOP))
        for mask in (FIRST ^ SECOND, one, two, 0):
            starts += [to_core * half + jnp.bitwise_xor(z, mask) * width + s for s in range(0, width, TILE)]
    return starts


def ring_plan(zs, scale, slab, factor_one, factor_two):
    half = factor_two.shape[1] // CORES
    starts = functools.partial(ring_starts, half, half // zs)
    parts = project(slab, factor_one, factor_two, starts, 2 * zs)
    passed, given, across, own = (o + swap(t, "core") for t, o in zip(parts[:zs], parts[zs:]))
    arrived = hop(passed, zs, FIRST_HOP)
    beside = hop(given, zs, FIRST_HOP)
    onward = across + arrived
    far_add = hop(onward, zs, SECOND_HOP, flip=1)
    own_add = hop(onward, zs, SECOND_HOP)
    own = lax.optimization_barrier((own, onward))[0] + beside
    blocks, flag = gram_blocks((own, own_add), (swap(own, "col"), far_add), zs, scale)
    blocks = blocks + swap(blocks, "core")
    pair = blocks[:2] + hop(blocks[2:], zs, (FIRST, FIRST), cross=1)
    last = pair[0] + hop(pair[1], zs, (SECOND, SECOND), cross=1)
    depth, rows = slab.shape[0], last.shape[0] // CORES
    return jnp.where(flag[:rows, :depth] == 1, last[rows:, :depth], last[:rows, :depth]).T


def general_plan(scale, slab, factor_one, factor_two):
    depth = slab.shape[0]
    r1, r2 = factor_one.shape[1], factor_two.shape[1]
    half = r2 // CORES

    def starts():
        core = lax.axis_index("core")
        return [side * half + s for side in (1 - core, core) for s in range(0, half, TILE)]

    other, own = project(slab, factor_one, factor_two, starts, 2)
    own = own + swap(other, "core")
    own = own.transpose(0, 2, 1, 3).reshape(half, depth, r1)
    share = lax.psum_scatter(own, "z", scatter_dimension=0, tiled=True)
    whole = lax.all_gather(share, "col", axis=1, tiled=True)
    gram = jnp.einsum("skr,slr->kl", share, whole, precision=lax.Precision.HIGHEST)
    return lax.psum_scatter(gram, ("z", "core"), scatter_dimension=1, tiled=True) * scale


def per_device(zs, cols, slab, factor_one, factor_two):
    r1, r2 = factor_one.shape[1], factor_two.shape[1]
    scale = 1.0 / (r1 * r2)
    depth = slab.shape[0]
    if zs == RING and cols == 2 and r2 % (CORES * zs * TILE) == 0 and cols * depth == zs * TILE:
        return ring_plan(zs, scale, slab, factor_one, factor_two)
    return general_plan(scale, slab, factor_one, factor_two)


def solution(mesh):
    groups, rows, cols = mesh.devices.shape
    zs = rows // CORES
    fine = Mesh(mesh.devices.reshape(groups, zs, CORES, cols), ("groups", "z", "core", "col"))
    row = ("z", "core")
    return jax.shard_map(
        functools.partial(per_device, zs, cols),
        mesh=fine,
        in_specs=(P(("groups", "col"), row, None), P(), P(row, None)),
        out_specs=P(("groups", "col"), row),
        check_vma=False,
    )
```

```python
import functools

import jax
import jax.numpy as jnp
from jax import lax
from jax.experimental import pallas as pl
from jax.experimental.pallas import tpu as pltpu
from jax.sharding import Mesh, PartitionSpec as P

TILE = 8
CORES = 2
CHUNK = 4
RING = 4
FIRST = 1
SECOND = 2


def project_kernel(chunk, starts, slab_ref, one_ref, two_ref, *rest):
    outs, (slab_buf, one_buf, two_buf, turned, sems) = rest[:-5], rest[-5:]
    depth, width, _ = slab_ref.shape
    chunks = depth // chunk
    copies = []
    for c in range(chunks):
        part = pl.ds(c * chunk, chunk)
        copies.append(pltpu.make_async_copy(slab_ref.at[part], slab_buf.at[part], sems.at[c]))
    copies[0].start()
    one_copy = pltpu.make_async_copy(one_ref, one_buf, sems.at[chunks])
    one_copy.start()
    two_copy = pltpu.make_async_copy(two_ref, two_buf, sems.at[chunks + 1])
    two_copy.start()
    for copy in copies[1:]:
        copy.start()
    two_copy.wait()
    turned[...] = two_buf[...].astype(jnp.float32).T
    pieces = [turned[pl.ds(pl.multiple_of(s, TILE), TILE), :] for s in starts()]
    two = jnp.concatenate(pieces, axis=0).astype(jnp.bfloat16)
    share = two.shape[0] // len(outs)

    def second(c, first):
        for q in range(chunk):
            core_part = jnp.dot(two, first[q * width : (q + 1) * width], preferred_element_type=jnp.float32)
            for o, out in enumerate(outs):
                piece = core_part[o * share : (o + 1) * share]
                out[:, c * chunk + q] = piece.reshape(share // TILE, TILE, -1)

    one_copy.wait()
    late = None
    for c in range(chunks):
        copies[c].wait()
        rows = slab_buf[pl.ds(c * chunk, chunk)].reshape(chunk * width, -1)
        middle = rows.shape[1] // 2
        first = jnp.dot(rows[:, :middle], one_buf[:middle], preferred_element_type=jnp.float32)
        first = first + jnp.dot(rows[:, middle:], one_buf[middle:], preferred_element_type=jnp.float32)
        first = first.astype(jnp.bfloat16)
        if late is not None:
            second(c - 1, late)
        late = first
    second(chunks - 1, late)


def project(slab, factor_one, factor_two, starts, outputs):
    depth, width, length = slab.shape
    r1, r2 = factor_one.shape[1], factor_two.shape[1]
    chunk = CHUNK if depth % CHUNK == 0 else 1
    out = pltpu.VMEM((r2 // TILE // outputs, depth, TILE, r1), jnp.float32)
    return pl.pallas_call(
        functools.partial(project_kernel, chunk, starts),
        out_shape=(out,) * outputs,
        in_specs=[pl.BlockSpec(memory_space=pltpu.HBM)] * 3,
        out_specs=[pl.BlockSpec(memory_space=pltpu.VMEM)] * outputs,
        scratch_shapes=[
            pltpu.VMEM(slab.shape, slab.dtype),
            pltpu.VMEM(factor_one.shape, factor_one.dtype),
            pltpu.VMEM(factor_two.shape, factor_two.dtype),
            pltpu.VMEM((r2, width), jnp.float32),
            pltpu.SemaphoreType.DMA((depth // chunk + 2,)),
        ],
        compiler_params=pltpu.CompilerParams(vmem_limit_bytes=32 * 2**20),
        cost_estimate=pl.CostEstimate(
            flops=2 * depth * width * r1 * (length + r2),
            bytes_accessed=2 * (slab.size + factor_one.size) + 4 * depth * r2 * r1,
            transcendentals=0,
        ),
    )(*(pltpu.with_memory_space_constraint(a, pltpu.HBM) for a in (slab, factor_one, factor_two)))


def gram_kernel(scale, own_ref, own_add, far_ref, far_add, out_ref, flag_ref, total, gram):
    groups, depth, tile, _ = own_ref.shape
    z, core, x = (lax.axis_index(name) for name in ("z", "core", "col"))
    chips, share, _ = out_ref.shape
    size = depth * tile
    value = jnp.zeros((2 * depth, depth), jnp.float32)
    for g in range(groups):
        total[g, pl.ds(pl.multiple_of(x * size, size), size), :] = (own_ref[g] + own_add[g]).reshape(size, -1)
        total[g, pl.ds(pl.multiple_of((1 - x) * size, size), size), :] = (far_ref[g] + far_add[g]).reshape(size, -1)
    picks = [(g, s) for g in range(groups) for s in range(tile)]
    for n in range(0, len(picks), 16):
        part = picks[n : n + 16]
        rows = jnp.concatenate([total[g, pl.ds(s, 2 * depth, stride=tile), :] for g, s in part], axis=1)
        own = jnp.concatenate([total[g, pl.ds(x * size + s, depth, stride=tile), :] for g, s in part], axis=1)
        value = value + lax.dot_general(
            rows,
            own,
            (((1,), (1,)), ((), ())),
            precision=lax.Precision.HIGHEST,
            preferred_element_type=jnp.float32,
        )
    gram[:, 0:depth] = value * scale
    for slot, hops in enumerate(((), (SECOND,), (FIRST,), (FIRST, SECOND))):
        to_z = z
        for hop in hops:
            to_z = jnp.bitwise_xor(to_z, hop)
        out_ref[slot] = gram[pl.ds(pl.multiple_of(to_z * share, TILE), share), :]
    flag_ref[...] = jnp.full(flag_ref.shape, core, jnp.int32)


def gram_blocks(own, far, chips, scale):
    groups, depth, tile, r1 = own[0].shape
    full = 2 * depth
    return pl.pallas_call(
        functools.partial(gram_kernel, scale),
        out_shape=(pltpu.VMEM((chips, full // chips, 128), jnp.float32), pltpu.VMEM((TILE, 128), jnp.int32)),
        in_specs=[pl.BlockSpec(memory_space=pltpu.VMEM)] * 4,
        out_specs=[pl.BlockSpec(memory_space=pltpu.VMEM)] * 2,
        scratch_shapes=[
            pltpu.VMEM((groups, full * tile, r1), jnp.float32),
            pltpu.VMEM((full, 128), jnp.float32),
        ],
        cost_estimate=pl.CostEstimate(
            flops=2 * groups * full * depth * tile * r1, bytes_accessed=16 * own[0].size, transcendentals=0
        ),
    )(*(pltpu.with_memory_space_constraint(a, pltpu.VMEM) for a in own + far))


def hop(value, zs, masks, cross=0, flip=0):
    pairs = []
    for z in range(zs):
        for core in range(CORES):
            for x in range(2):
                to = ((z ^ masks[core]) * CORES + (core ^ cross)) * 2 + (x ^ flip)
                pairs.append(((z * CORES + core) * 2 + x, to))
    return lax.ppermute(value, ("z", "core", "col"), pairs)


def swap(value, axis):
    return lax.ppermute(value, axis, [(0, 1), (1, 0)])


FIRST_HOP = (FIRST, SECOND)
SECOND_HOP = (SECOND, FIRST)


def ring_starts(half, width):
    z, core = lax.axis_index("z"), lax.axis_index("core")
    starts = []
    for to_core in (1 - core, core):
        one, two = (to_core * (hops[1] - hops[0]) + hops[0] for hops in (FIRST_HOP, SECOND_HOP))
        for mask in (FIRST ^ SECOND, one, two, 0):
            starts += [to_core * half + jnp.bitwise_xor(z, mask) * width + s for s in range(0, width, TILE)]
    return starts


def ring_plan(zs, scale, slab, factor_one, factor_two):
    half = factor_two.shape[1] // CORES
    starts = functools.partial(ring_starts, half, half // zs)
    parts = project(slab, factor_one, factor_two, starts, 2 * zs)
    passed, given, across, own = (o + swap(t, "core") for t, o in zip(parts[:zs], parts[zs:]))
    arrived = hop(passed, zs, FIRST_HOP)
    beside = hop(given, zs, FIRST_HOP)
    onward = across + arrived
    far_add = hop(onward, zs, SECOND_HOP, flip=1)
    own_add = hop(onward, zs, SECOND_HOP)
    own = lax.optimization_barrier((own, onward))[0] + beside
    blocks, flag = gram_blocks((own, own_add), (swap(own, "col"), far_add), zs, scale)
    blocks = blocks + swap(blocks, "core")
    pair = blocks[:2] + hop(blocks[2:], zs, (FIRST, FIRST), cross=1)
    last = pair[0] + hop(pair[1], zs, (SECOND, SECOND), cross=1)
    depth, rows = slab.shape[0], last.shape[0] // CORES
    return jnp.where(flag[:rows, :depth] == 1, last[rows:, :depth], last[:rows, :depth]).T


def general_plan(scale, slab, factor_one, factor_two):
    depth = slab.shape[0]
    r1, r2 = factor_one.shape[1], factor_two.shape[1]
    half = r2 // CORES

    def starts():
        core = lax.axis_index("core")
        return [side * half + s for side in (1 - core, core) for s in range(0, half, TILE)]

    other, own = project(slab, factor_one, factor_two, starts, 2)
    own = own + swap(other, "core")
    own = own.transpose(0, 2, 1, 3).reshape(half, depth, r1)
    share = lax.psum_scatter(own, "z", scatter_dimension=0, tiled=True)
    whole = lax.all_gather(share, "col", axis=1, tiled=True)
    gram = jnp.einsum("skr,slr->kl", share, whole, precision=lax.Precision.HIGHEST)
    return lax.psum_scatter(gram, ("z", "core"), scatter_dimension=1, tiled=True) * scale


def per_device(zs, cols, slab, factor_one, factor_two):
    r1, r2 = factor_one.shape[1], factor_two.shape[1]
    scale = 1.0 / (r1 * r2)
    depth = slab.shape[0]
    if zs == RING and cols == 2 and r2 % (CORES * zs * TILE) == 0 and cols * depth == zs * TILE:
        return ring_plan(zs, scale, slab, factor_one, factor_two)
    return general_plan(scale, slab, factor_one, factor_two)


def solution(mesh):
    groups, rows, cols = mesh.devices.shape
    zs = rows // CORES
    fine = Mesh(mesh.devices.reshape(groups, zs, CORES, cols), ("groups", "z", "core", "col"))
    row = ("z", "core")
    return jax.shard_map(
        functools.partial(per_device, zs, cols),
        mesh=fine,
        in_specs=(P(("groups", "col"), row, None), P(), P(row, None)),
        out_specs=P(("groups", "col"), row),
        check_vma=False,
    )
```

```python
import functools

import jax
import jax.numpy as jnp
from jax import lax
from jax.experimental import pallas as pl
from jax.experimental.pallas import tpu as pltpu
from jax.sharding import Mesh, PartitionSpec as P

TILE = 8
CORES = 2
CHUNK = 4
RING = 4
FIRST = 1
SECOND = 2


def project_kernel(chunk, starts, slab_ref, one_ref, two_ref, *rest):
    outs, (slab_buf, one_buf, two_buf, turned, sems) = rest[:-5], rest[-5:]
    depth, width, _ = slab_ref.shape
    chunks = depth // chunk
    copies = []
    for c in range(chunks):
        part = pl.ds(c * chunk, chunk)
        copies.append(pltpu.make_async_copy(slab_ref.at[part], slab_buf.at[part], sems.at[c]))
    copies[0].start()
    one_copy = pltpu.make_async_copy(one_ref, one_buf, sems.at[chunks])
    one_copy.start()
    two_copy = pltpu.make_async_copy(two_ref, two_buf, sems.at[chunks + 1])
    two_copy.start()
    for copy in copies[1:]:
        copy.start()
    two_copy.wait()
    turned[...] = two_buf[...].astype(jnp.float32).T
    pieces = [turned[pl.ds(pl.multiple_of(s, TILE), TILE), :] for s in starts()]
    two = jnp.concatenate(pieces, axis=0).astype(jnp.bfloat16)
    share = two.shape[0] // len(outs)

    def second(c, first):
        for q in range(chunk):
            core_part = jnp.dot(two, first[q * width : (q + 1) * width], preferred_element_type=jnp.float32)
            for o, out in enumerate(outs):
                piece = core_part[o * share : (o + 1) * share]
                out[:, c * chunk + q] = piece.reshape(share // TILE, TILE, -1)

    one_copy.wait()
    late = None
    for c in range(chunks):
        copies[c].wait()
        rows = slab_buf[pl.ds(c * chunk, chunk)].reshape(chunk * width, -1)
        middle = rows.shape[1] // 2
        first = jnp.dot(rows[:, :middle], one_buf[:middle], preferred_element_type=jnp.float32)
        first = first + jnp.dot(rows[:, middle:], one_buf[middle:], preferred_element_type=jnp.float32)
        first = first.astype(jnp.bfloat16)
        if late is not None:
            second(c - 1, late)
        late = first
    second(chunks - 1, late)


def project(slab, factor_one, factor_two, starts, outputs):
    depth, width, length = slab.shape
    r1, r2 = factor_one.shape[1], factor_two.shape[1]
    chunk = CHUNK if depth % CHUNK == 0 else 1
    out = pltpu.VMEM((r2 // TILE // outputs, depth, TILE, r1), jnp.float32)
    return pl.pallas_call(
        functools.partial(project_kernel, chunk, starts),
        out_shape=(out,) * outputs,
        in_specs=[pl.BlockSpec(memory_space=pltpu.HBM)] * 3,
        out_specs=[pl.BlockSpec(memory_space=pltpu.VMEM)] * outputs,
        scratch_shapes=[
            pltpu.VMEM(slab.shape, slab.dtype),
            pltpu.VMEM(factor_one.shape, factor_one.dtype),
            pltpu.VMEM(factor_two.shape, factor_two.dtype),
            pltpu.VMEM((r2, width), jnp.float32),
            pltpu.SemaphoreType.DMA((depth // chunk + 2,)),
        ],
        compiler_params=pltpu.CompilerParams(vmem_limit_bytes=32 * 2**20),
        cost_estimate=pl.CostEstimate(
            flops=2 * depth * width * r1 * (length + r2),
            bytes_accessed=2 * (slab.size + factor_one.size) + 4 * depth * r2 * r1,
            transcendentals=0,
        ),
    )(*(pltpu.with_memory_space_constraint(a, pltpu.HBM) for a in (slab, factor_one, factor_two)))


def halves(value):
    high = value.astype(jnp.bfloat16)
    low = (value - high.astype(jnp.float32)).astype(jnp.bfloat16)
    return jnp.concatenate([high, low], axis=0)


def gram_kernel(scale, own_ref, own_add, far_ref, far_add, out_ref, flag_ref, total, gram):
    groups, depth, tile, _ = own_ref.shape
    z, core, x = (lax.axis_index(name) for name in ("z", "core", "col"))
    chips, share, _ = out_ref.shape
    size = depth * tile
    value = jnp.zeros((2 * depth, depth), jnp.float32)
    for g in range(groups):
        total[g, pl.ds(pl.multiple_of(x * size, size), size), :] = (own_ref[g] + own_add[g]).reshape(size, -1)
        total[g, pl.ds(pl.multiple_of((1 - x) * size, size), size), :] = (far_ref[g] + far_add[g]).reshape(size, -1)
    picks = [(g, s) for g in range(groups) for s in range(tile)]
    for n in range(0, len(picks), 16):
        part = picks[n : n + 16]
        rows = jnp.concatenate([total[g, pl.ds(s, 2 * depth, stride=tile), :] for g, s in part], axis=1)
        own = jnp.concatenate([total[g, pl.ds(x * size + s, depth, stride=tile), :] for g, s in part], axis=1)
        four = lax.dot_general(
            halves(rows), halves(own), (((1,), (1,)), ((), ())), preferred_element_type=jnp.float32
        )
        for at in (0, 2 * depth):
            value = value + (four[at : at + 2 * depth, 0:depth] + four[at : at + 2 * depth, depth : 2 * depth])
    gram[:, 0:depth] = value * scale
    for slot, hops in enumerate(((), (SECOND,), (FIRST,), (FIRST, SECOND))):
        to_z = z
        for hop in hops:
            to_z = jnp.bitwise_xor(to_z, hop)
        out_ref[slot] = gram[pl.ds(pl.multiple_of(to_z * share, TILE), share), :]
    flag_ref[...] = jnp.full(flag_ref.shape, core, jnp.int32)


def gram_blocks(own, far, chips, scale):
    groups, depth, tile, r1 = own[0].shape
    full = 2 * depth
    return pl.pallas_call(
        functools.partial(gram_kernel, scale),
        out_shape=(pltpu.VMEM((chips, full // chips, 128), jnp.float32), pltpu.VMEM((TILE, 128), jnp.int32)),
        in_specs=[pl.BlockSpec(memory_space=pltpu.VMEM)] * 4,
        out_specs=[pl.BlockSpec(memory_space=pltpu.VMEM)] * 2,
        scratch_shapes=[
            pltpu.VMEM((groups, full * tile, r1), jnp.float32),
            pltpu.VMEM((full, 128), jnp.float32),
        ],
        cost_estimate=pl.CostEstimate(
            flops=2 * groups * full * depth * tile * r1, bytes_accessed=16 * own[0].size, transcendentals=0
        ),
    )(*(pltpu.with_memory_space_constraint(a, pltpu.VMEM) for a in own + far))


def hop(value, zs, masks, cross=0, flip=0):
    pairs = []
    for z in range(zs):
        for core in range(CORES):
            for x in range(2):
                to = ((z ^ masks[core]) * CORES + (core ^ cross)) * 2 + (x ^ flip)
                pairs.append(((z * CORES + core) * 2 + x, to))
    return lax.ppermute(value, ("z", "core", "col"), pairs)


def swap(value, axis):
    return lax.ppermute(value, axis, [(0, 1), (1, 0)])


FIRST_HOP = (FIRST, SECOND)
SECOND_HOP = (SECOND, FIRST)


def ring_starts(half, width):
    z, core = lax.axis_index("z"), lax.axis_index("core")
    starts = []
    for to_core in (1 - core, core):
        one, two = (to_core * (hops[1] - hops[0]) + hops[0] for hops in (FIRST_HOP, SECOND_HOP))
        for mask in (FIRST ^ SECOND, one, two, 0):
            starts += [to_core * half + jnp.bitwise_xor(z, mask) * width + s for s in range(0, width, TILE)]
    return starts


def ring_plan(zs, scale, slab, factor_one, factor_two):
    half = factor_two.shape[1] // CORES
    starts = functools.partial(ring_starts, half, half // zs)
    parts = project(slab, factor_one, factor_two, starts, 2 * zs)
    passed, given, across, own = (o + swap(t, "core") for t, o in zip(parts[:zs], parts[zs:]))
    arrived = hop(passed, zs, FIRST_HOP)
    beside = hop(given, zs, FIRST_HOP)
    onward = across + arrived
    far_add = hop(onward, zs, SECOND_HOP, flip=1)
    own_add = hop(onward, zs, SECOND_HOP)
    own = lax.optimization_barrier((own, onward))[0] + beside
    blocks, flag = gram_blocks((own, own_add), (swap(own, "col"), far_add), zs, scale)
    blocks = blocks + swap(blocks, "core")
    pair = blocks[:2] + hop(blocks[2:], zs, (FIRST, FIRST), cross=1)
    last = pair[0] + hop(pair[1], zs, (SECOND, SECOND), cross=1)
    depth, rows = slab.shape[0], last.shape[0] // CORES
    return jnp.where(flag[:rows, :depth] == 1, last[rows:, :depth], last[:rows, :depth]).T


def general_plan(scale, slab, factor_one, factor_two):
    depth = slab.shape[0]
    r1, r2 = factor_one.shape[1], factor_two.shape[1]
    half = r2 // CORES

    def starts():
        core = lax.axis_index("core")
        return [side * half + s for side in (1 - core, core) for s in range(0, half, TILE)]

    other, own = project(slab, factor_one, factor_two, starts, 2)
    own = own + swap(other, "core")
    own = own.transpose(0, 2, 1, 3).reshape(half, depth, r1)
    share = lax.psum_scatter(own, "z", scatter_dimension=0, tiled=True)
    whole = lax.all_gather(share, "col", axis=1, tiled=True)
    gram = jnp.einsum("skr,slr->kl", share, whole, precision=lax.Precision.HIGHEST)
    return lax.psum_scatter(gram, ("z", "core"), scatter_dimension=1, tiled=True) * scale


def per_device(zs, cols, slab, factor_one, factor_two):
    r1, r2 = factor_one.shape[1], factor_two.shape[1]
    scale = 1.0 / (r1 * r2)
    depth = slab.shape[0]
    if zs == RING and cols == 2 and r2 % (CORES * zs * TILE) == 0 and cols * depth == zs * TILE:
        return ring_plan(zs, scale, slab, factor_one, factor_two)
    return general_plan(scale, slab, factor_one, factor_two)


def solution(mesh):
    groups, rows, cols = mesh.devices.shape
    zs = rows // CORES
    fine = Mesh(mesh.devices.reshape(groups, zs, CORES, cols), ("groups", "z", "core", "col"))
    row = ("z", "core")
    return jax.shard_map(
        functools.partial(per_device, zs, cols),
        mesh=fine,
        in_specs=(P(("groups", "col"), row, None), P(), P(row, None)),
        out_specs=P(("groups", "col"), row),
        check_vma=False,
    )
```

```python
import functools

import jax
import jax.numpy as jnp
from jax import lax
from jax.experimental import pallas as pl
from jax.experimental.pallas import tpu as pltpu
from jax.sharding import Mesh, PartitionSpec as P

TILE = 8
CORES = 2
CHUNK = 4
RING = 4
FIRST = 1
SECOND = 2


def project_kernel(chunk, starts, slab_ref, one_ref, two_ref, *rest):
    outs, (slab_buf, one_buf, two_buf, turned, sems) = rest[:-5], rest[-5:]
    depth, width, _ = slab_ref.shape
    chunks = depth // chunk
    copies = []
    for c in range(chunks):
        part = pl.ds(c * chunk, chunk)
        copies.append(pltpu.make_async_copy(slab_ref.at[part], slab_buf.at[part], sems.at[c]))
    copies[0].start()
    one_copy = pltpu.make_async_copy(one_ref, one_buf, sems.at[chunks])
    one_copy.start()
    two_copy = pltpu.make_async_copy(two_ref, two_buf, sems.at[chunks + 1])
    two_copy.start()
    for copy in copies[1:]:
        copy.start()
    two_copy.wait()
    turned[...] = two_buf[...].astype(jnp.float32).T
    pieces = [turned[pl.ds(pl.multiple_of(s, TILE), TILE), :] for s in starts()]
    two = jnp.concatenate(pieces, axis=0).astype(jnp.bfloat16)
    share = two.shape[0] // len(outs)

    def second(c, first):
        for q in range(chunk):
            core_part = jnp.dot(two, first[q * width : (q + 1) * width], preferred_element_type=jnp.float32)
            for o, out in enumerate(outs):
                piece = core_part[o * share : (o + 1) * share]
                out[:, c * chunk + q] = piece.reshape(share // TILE, TILE, -1)

    one_copy.wait()
    late = None
    for c in range(chunks):
        copies[c].wait()
        rows = slab_buf[pl.ds(c * chunk, chunk)].reshape(chunk * width, -1)
        middle = rows.shape[1] // 2
        first = jnp.dot(rows[:, :middle], one_buf[:middle], preferred_element_type=jnp.float32)
        first = first + jnp.dot(rows[:, middle:], one_buf[middle:], preferred_element_type=jnp.float32)
        first = first.astype(jnp.bfloat16)
        if late is not None:
            second(c - 1, late)
        late = first
    second(chunks - 1, late)


def project(slab, factor_one, factor_two, starts, outputs):
    depth, width, length = slab.shape
    r1, r2 = factor_one.shape[1], factor_two.shape[1]
    chunk = CHUNK if depth % CHUNK == 0 else 1
    out = pltpu.VMEM((r2 // TILE // outputs, depth, TILE, r1), jnp.float32)
    return pl.pallas_call(
        functools.partial(project_kernel, chunk, starts),
        out_shape=(out,) * outputs,
        in_specs=[pl.BlockSpec(memory_space=pltpu.HBM)] * 3,
        out_specs=[pl.BlockSpec(memory_space=pltpu.VMEM)] * outputs,
        scratch_shapes=[
            pltpu.VMEM(slab.shape, slab.dtype),
            pltpu.VMEM(factor_one.shape, factor_one.dtype),
            pltpu.VMEM(factor_two.shape, factor_two.dtype),
            pltpu.VMEM((r2, width), jnp.float32),
            pltpu.SemaphoreType.DMA((depth // chunk + 2,)),
        ],
        compiler_params=pltpu.CompilerParams(vmem_limit_bytes=32 * 2**20),
        cost_estimate=pl.CostEstimate(
            flops=2 * depth * width * r1 * (length + r2),
            bytes_accessed=2 * (slab.size + factor_one.size) + 4 * depth * r2 * r1,
            transcendentals=0,
        ),
    )(*(pltpu.with_memory_space_constraint(a, pltpu.HBM) for a in (slab, factor_one, factor_two)))


def halves(value):
    high = value.astype(jnp.bfloat16)
    low = (value - high.astype(jnp.float32)).astype(jnp.bfloat16)
    return jnp.concatenate([high, low], axis=0)


def gram_kernel(scale, own_ref, own_add, far_ref, far_add, out_ref, flag_ref, total, gram):
    groups, depth, tile, _ = own_ref.shape
    z, core, x = (lax.axis_index(name) for name in ("z", "core", "col"))
    chips, share, _ = out_ref.shape
    size = depth * tile
    value = jnp.zeros((2 * depth, depth), jnp.float32)
    for g in range(groups):
        total[g, pl.ds(pl.multiple_of(x * size, size), size), :] = (own_ref[g] + own_add[g]).reshape(size, -1)
        total[g, pl.ds(pl.multiple_of((1 - x) * size, size), size), :] = (far_ref[g] + far_add[g]).reshape(size, -1)
    picks = [(g, s) for g in range(groups) for s in range(tile)]
    for n in range(0, len(picks), 16):
        part = picks[n : n + 16]
        rows = jnp.concatenate([total[g, pl.ds(s, 2 * depth, stride=tile), :] for g, s in part], axis=1)
        own = jnp.concatenate([total[g, pl.ds(x * size + s, depth, stride=tile), :] for g, s in part], axis=1)
        four = lax.dot_general(
            halves(rows), halves(own), (((1,), (1,)), ((), ())), preferred_element_type=jnp.float32
        )
        for at in (0, 2 * depth):
            value = value + (four[at : at + 2 * depth, 0:depth] + four[at : at + 2 * depth, depth : 2 * depth])
    gram[:, 0:depth] = value * scale
    for slot, hops in enumerate(((), (SECOND,), (FIRST,), (FIRST, SECOND))):
        to_z = z
        for hop in hops:
            to_z = jnp.bitwise_xor(to_z, hop)
        out_ref[slot] = gram[pl.ds(pl.multiple_of(to_z * share, TILE), share), :]
    flag_ref[...] = jnp.full(flag_ref.shape, core, jnp.int32)


def gram_blocks(own, far, chips, scale):
    groups, depth, tile, r1 = own[0].shape
    full = 2 * depth
    return pl.pallas_call(
        functools.partial(gram_kernel, scale),
        out_shape=(pltpu.VMEM((chips, full // chips, 128), jnp.float32), pltpu.VMEM((TILE, 128), jnp.int32)),
        in_specs=[pl.BlockSpec(memory_space=pltpu.VMEM)] * 4,
        out_specs=[pl.BlockSpec(memory_space=pltpu.VMEM)] * 2,
        scratch_shapes=[
            pltpu.VMEM((groups, full * tile, r1), jnp.float32),
            pltpu.VMEM((full, 128), jnp.float32),
        ],
        cost_estimate=pl.CostEstimate(
            flops=2 * groups * full * depth * tile * r1, bytes_accessed=16 * own[0].size, transcendentals=0
        ),
    )(*(pltpu.with_memory_space_constraint(a, pltpu.VMEM) for a in own + far))


def hop(value, zs, masks, cross=0, flip=0):
    pairs = []
    for z in range(zs):
        for core in range(CORES):
            for x in range(2):
                to = ((z ^ masks[core]) * CORES + (core ^ cross)) * 2 + (x ^ flip)
                pairs.append(((z * CORES + core) * 2 + x, to))
    return lax.ppermute(value, ("z", "core", "col"), pairs)


def swap(value, axis):
    return lax.ppermute(value, axis, [(0, 1), (1, 0)])


FIRST_HOP = (FIRST, SECOND)
SECOND_HOP = (SECOND, FIRST)


def ring_starts(half, width):
    z, core = lax.axis_index("z"), lax.axis_index("core")
    starts = []
    for to_core in (1 - core, core):
        one, two = (to_core * (hops[1] - hops[0]) + hops[0] for hops in (FIRST_HOP, SECOND_HOP))
        for mask in (FIRST ^ SECOND, one, two, 0):
            starts += [to_core * half + jnp.bitwise_xor(z, mask) * width + s for s in range(0, width, TILE)]
    return starts


def ring_plan(zs, scale, slab, factor_one, factor_two):
    half = factor_two.shape[1] // CORES
    starts = functools.partial(ring_starts, half, half // zs)
    parts = project(slab, factor_one, factor_two, starts, 2 * zs)
    passed, given, across, own = (o + swap(t, "core") for t, o in zip(parts[:zs], parts[zs:]))
    arrived = hop(passed, zs, FIRST_HOP)
    beside = hop(given, zs, FIRST_HOP)
    onward = across + arrived
    far_add = hop(onward, zs, SECOND_HOP, flip=1)
    own_add = hop(onward, zs, SECOND_HOP)
    own = lax.optimization_barrier((own, onward))[0] + beside
    blocks, flag = gram_blocks((own, own_add), (swap(own, "col"), far_add), zs, scale)
    pair = blocks[0::2] + hop(blocks[1::2], zs, (SECOND, SECOND), cross=1)
    pair = pair + swap(pair, "core")
    last = pair[0] + hop(pair[1], zs, (FIRST, FIRST), cross=1)
    depth, rows = slab.shape[0], last.shape[0] // CORES
    return jnp.where(flag[:rows, :depth] == 1, last[rows:, :depth], last[:rows, :depth]).T


def general_plan(scale, slab, factor_one, factor_two):
    depth = slab.shape[0]
    r1, r2 = factor_one.shape[1], factor_two.shape[1]
    half = r2 // CORES

    def starts():
        core = lax.axis_index("core")
        return [side * half + s for side in (1 - core, core) for s in range(0, half, TILE)]

    other, own = project(slab, factor_one, factor_two, starts, 2)
    own = own + swap(other, "core")
    own = own.transpose(0, 2, 1, 3).reshape(half, depth, r1)
    share = lax.psum_scatter(own, "z", scatter_dimension=0, tiled=True)
    whole = lax.all_gather(share, "col", axis=1, tiled=True)
    gram = jnp.einsum("skr,slr->kl", share, whole, precision=lax.Precision.HIGHEST)
    return lax.psum_scatter(gram, ("z", "core"), scatter_dimension=1, tiled=True) * scale


def per_device(zs, cols, slab, factor_one, factor_two):
    r1, r2 = factor_one.shape[1], factor_two.shape[1]
    scale = 1.0 / (r1 * r2)
    depth = slab.shape[0]
    if zs == RING and cols == 2 and r2 % (CORES * zs * TILE) == 0 and cols * depth == zs * TILE:
        return ring_plan(zs, scale, slab, factor_one, factor_two)
    return general_plan(scale, slab, factor_one, factor_two)


def solution(mesh):
    groups, rows, cols = mesh.devices.shape
    zs = rows // CORES
    fine = Mesh(mesh.devices.reshape(groups, zs, CORES, cols), ("groups", "z", "core", "col"))
    row = ("z", "core")
    return jax.shard_map(
        functools.partial(per_device, zs, cols),
        mesh=fine,
        in_specs=(P(("groups", "col"), row, None), P(), P(row, None)),
        out_specs=P(("groups", "col"), row),
        check_vma=False,
    )
```

```python
import functools

import jax
import jax.numpy as jnp
from jax import lax
from jax.experimental import pallas as pl
from jax.experimental.pallas import tpu as pltpu
from jax.sharding import Mesh, PartitionSpec as P

TILE = 8
CORES = 2
CHUNK = 4
RING = 4
FIRST = 1
SECOND = 2


def project_kernel(chunk, starts, slab_ref, one_ref, two_ref, *rest):
    outs, (slab_buf, one_buf, two_buf, turned, sems) = rest[:-5], rest[-5:]
    depth, width, _ = slab_ref.shape
    chunks = depth // chunk
    copies = []
    for c in range(chunks):
        part = pl.ds(c * chunk, chunk)
        copies.append(pltpu.make_async_copy(slab_ref.at[part], slab_buf.at[part], sems.at[c]))
    copies[0].start()
    one_copy = pltpu.make_async_copy(one_ref, one_buf, sems.at[chunks])
    one_copy.start()
    two_copy = pltpu.make_async_copy(two_ref, two_buf, sems.at[chunks + 1])
    two_copy.start()
    for copy in copies[1:]:
        copy.start()
    two_copy.wait()
    turned[...] = two_buf[...].astype(jnp.float32).T
    pieces = [turned[pl.ds(pl.multiple_of(s, TILE), TILE), :] for s in starts()]
    two = jnp.concatenate(pieces, axis=0).astype(jnp.bfloat16)
    share = two.shape[0] // len(outs)

    def second(c, first):
        for q in range(chunk):
            core_part = jnp.dot(two, first[q * width : (q + 1) * width], preferred_element_type=jnp.float32)
            for o, out in enumerate(outs):
                piece = core_part[o * share : (o + 1) * share]
                out[:, c * chunk + q] = piece.reshape(share // TILE, TILE, -1)

    one_copy.wait()
    late = None
    for c in range(chunks):
        copies[c].wait()
        rows = slab_buf[pl.ds(c * chunk, chunk)].reshape(chunk * width, -1)
        middle = rows.shape[1] // 2
        first = jnp.dot(rows[:, :middle], one_buf[:middle], preferred_element_type=jnp.float32)
        first = first + jnp.dot(rows[:, middle:], one_buf[middle:], preferred_element_type=jnp.float32)
        first = first.astype(jnp.bfloat16)
        if late is not None:
            second(c - 1, late)
        late = first
    second(chunks - 1, late)


def project(slab, factor_one, factor_two, starts, outputs):
    depth, width, length = slab.shape
    r1, r2 = factor_one.shape[1], factor_two.shape[1]
    chunk = CHUNK if depth % CHUNK == 0 else 1
    out = pltpu.VMEM((r2 // TILE // outputs, depth, TILE, r1), jnp.float32)
    return pl.pallas_call(
        functools.partial(project_kernel, chunk, starts),
        out_shape=(out,) * outputs,
        in_specs=[pl.BlockSpec(memory_space=pltpu.HBM)] * 3,
        out_specs=[pl.BlockSpec(memory_space=pltpu.VMEM)] * outputs,
        scratch_shapes=[
            pltpu.VMEM(slab.shape, slab.dtype),
            pltpu.VMEM(factor_one.shape, factor_one.dtype),
            pltpu.VMEM(factor_two.shape, factor_two.dtype),
            pltpu.VMEM((r2, width), jnp.float32),
            pltpu.SemaphoreType.DMA((depth // chunk + 2,)),
        ],
        compiler_params=pltpu.CompilerParams(vmem_limit_bytes=32 * 2**20),
        cost_estimate=pl.CostEstimate(
            flops=2 * depth * width * r1 * (length + r2),
            bytes_accessed=2 * (slab.size + factor_one.size) + 4 * depth * r2 * r1,
            transcendentals=0,
        ),
    )(*(pltpu.with_memory_space_constraint(a, pltpu.HBM) for a in (slab, factor_one, factor_two)))


def gram_kernel(scale, own_ref, own_add, far_ref, far_add, out_ref, flag_ref, total):
    groups, depth, tile, _ = own_ref.shape
    z, core, x = (lax.axis_index(name) for name in ("z", "core", "col"))
    chips, share, _ = out_ref.shape
    size = depth * tile
    for g in range(groups):
        total[g, 0:size, :] = (own_ref[g] + own_add[g]).reshape(size, -1)
        total[g, size : 2 * size, :] = (far_ref[g] + far_add[g]).reshape(size, -1)
    picks = [total[g, pl.ds(s, 2 * depth, stride=tile), :] for g in range(groups) for s in range(tile)]
    rows = jnp.concatenate(picks, axis=1)
    high = rows.astype(jnp.bfloat16)
    low = (rows - high.astype(jnp.float32)).astype(jnp.bfloat16)
    four = lax.dot_general(
        jnp.concatenate([high, low], axis=0),
        jnp.concatenate([high[0:depth], low[0:depth]], axis=0),
        (((1,), (1,)), ((), ())),
        preferred_element_type=jnp.float32,
    )
    value = (four[0 : 2 * depth, 0:depth] + four[0 : 2 * depth, depth : 2 * depth]) + (
        four[2 * depth : 4 * depth, 0:depth] + four[2 * depth : 4 * depth, depth : 2 * depth]
    )
    value = value * scale
    for n in range(chips):
        half, part = n // 2, n % 2
        mask = jnp.bitwise_xor(z, 2 * (x if half == 0 else 1 - x) + part)
        slot = mask // SECOND + 2 * (mask % SECOND)
        out_ref[slot, :, 0:depth] = value[n * share : (n + 1) * share]
    flag_ref[...] = jnp.full(flag_ref.shape, core, jnp.int32)


def gram_blocks(own, far, chips, scale):
    groups, depth, tile, r1 = own[0].shape
    full = 2 * depth
    return pl.pallas_call(
        functools.partial(gram_kernel, scale),
        out_shape=(pltpu.VMEM((chips, full // chips, 128), jnp.float32), pltpu.VMEM((TILE, 128), jnp.int32)),
        in_specs=[pl.BlockSpec(memory_space=pltpu.VMEM)] * 4,
        out_specs=[pl.BlockSpec(memory_space=pltpu.VMEM)] * 2,
        scratch_shapes=[
            pltpu.VMEM((groups, full * tile, r1), jnp.float32),
        ],
        cost_estimate=pl.CostEstimate(
            flops=2 * groups * full * depth * tile * r1, bytes_accessed=16 * own[0].size, transcendentals=0
        ),
    )(*(pltpu.with_memory_space_constraint(a, pltpu.VMEM) for a in own + far))


def hop(value, zs, masks, cross=0, flip=0):
    pairs = []
    for z in range(zs):
        for core in range(CORES):
            for x in range(2):
                to = ((z ^ masks[core]) * CORES + (core ^ cross)) * 2 + (x ^ flip)
                pairs.append(((z * CORES + core) * 2 + x, to))
    return lax.ppermute(value, ("z", "core", "col"), pairs)


def swap(value, axis):
    return lax.ppermute(value, axis, [(0, 1), (1, 0)])


FIRST_HOP = (FIRST, SECOND)
SECOND_HOP = (SECOND, FIRST)


def ring_starts(half, width):
    z, core = lax.axis_index("z"), lax.axis_index("core")
    starts = []
    for to_core in (1 - core, core):
        one, two = (to_core * (hops[1] - hops[0]) + hops[0] for hops in (FIRST_HOP, SECOND_HOP))
        for mask in (FIRST ^ SECOND, one, two, 0):
            starts += [to_core * half + jnp.bitwise_xor(z, mask) * width + s for s in range(0, width, TILE)]
    return starts


def ring_plan(zs, scale, slab, factor_one, factor_two):
    half = factor_two.shape[1] // CORES
    starts = functools.partial(ring_starts, half, half // zs)
    parts = project(slab, factor_one, factor_two, starts, 2 * zs)
    passed, given, across, own = (o + swap(t, "core") for t, o in zip(parts[:zs], parts[zs:]))
    arrived = hop(passed, zs, FIRST_HOP)
    beside = hop(given, zs, FIRST_HOP)
    onward = across + arrived
    own_add = hop(onward, zs, SECOND_HOP)
    far_add = hop(onward, zs, SECOND_HOP, flip=1)
    own = lax.optimization_barrier((own, onward))[0] + beside
    blocks, flag = gram_blocks((own, own_add), (swap(own, "col"), far_add), zs, scale)
    pair = blocks[0::2] + hop(blocks[1::2], zs, (SECOND, SECOND), cross=1)
    pair = pair + swap(pair, "core")
    last = pair[0] + hop(pair[1], zs, (FIRST, FIRST), cross=1)
    depth, rows = slab.shape[0], last.shape[0] // CORES
    return jnp.where(flag[:rows, :depth] == 1, last[rows:, :depth], last[:rows, :depth]).T


def general_plan(scale, slab, factor_one, factor_two):
    depth = slab.shape[0]
    r1, r2 = factor_one.shape[1], factor_two.shape[1]
    half = r2 // CORES

    def starts():
        core = lax.axis_index("core")
        return [side * half + s for side in (1 - core, core) for s in range(0, half, TILE)]

    other, own = project(slab, factor_one, factor_two, starts, 2)
    own = own + swap(other, "core")
    own = own.transpose(0, 2, 1, 3).reshape(half, depth, r1)
    share = lax.psum_scatter(own, "z", scatter_dimension=0, tiled=True)
    whole = lax.all_gather(share, "col", axis=1, tiled=True)
    gram = jnp.einsum("skr,slr->kl", share, whole, precision=lax.Precision.HIGHEST)
    return lax.psum_scatter(gram, ("z", "core"), scatter_dimension=1, tiled=True) * scale


def per_device(zs, cols, slab, factor_one, factor_two):
    r1, r2 = factor_one.shape[1], factor_two.shape[1]
    scale = 1.0 / (r1 * r2)
    depth = slab.shape[0]
    if zs == RING and cols == 2 and r2 % (CORES * zs * TILE) == 0 and cols * depth == zs * TILE:
        return ring_plan(zs, scale, slab, factor_one, factor_two)
    return general_plan(scale, slab, factor_one, factor_two)


def solution(mesh):
    groups, rows, cols = mesh.devices.shape
    zs = rows // CORES
    fine = Mesh(mesh.devices.reshape(groups, zs, CORES, cols), ("groups", "z", "core", "col"))
    row = ("z", "core")
    return jax.shard_map(
        functools.partial(per_device, zs, cols),
        mesh=fine,
        in_specs=(P(("groups", "col"), row, None), P(), P(row, None)),
        out_specs=P(("groups", "col"), row),
        check_vma=False,
    )
```

```python
import functools

import jax
import jax.numpy as jnp
from jax import lax
from jax.experimental import pallas as pl
from jax.experimental.pallas import tpu as pltpu
from jax.sharding import Mesh, PartitionSpec as P

TILE = 8
CORES = 2
CHUNK = 4
RING = 4
FIRST = 1
SECOND = 2


def project_kernel(chunk, starts, slab_ref, one_ref, two_ref, *rest):
    outs, (slab_buf, one_buf, two_buf, turned, sems) = rest[:-5], rest[-5:]
    depth, width, _ = slab_ref.shape
    r1 = one_ref.shape[1]
    chunks = depth // chunk
    copies = []
    for c in range(chunks):
        part = pl.ds(c * chunk, chunk)
        copies.append(pltpu.make_async_copy(slab_ref.at[part], slab_buf.at[part], sems.at[c]))
    copies[0].start()
    one_copy = pltpu.make_async_copy(one_ref, one_buf, sems.at[chunks])
    one_copy.start()
    two_copy = pltpu.make_async_copy(two_ref, two_buf, sems.at[chunks + 1])
    two_copy.start()
    for copy in copies[1:]:
        copy.start()
    two_copy.wait()
    turned[...] = two_buf[...].astype(jnp.float32).T
    pieces = [turned[pl.ds(pl.multiple_of(s, TILE), TILE), :] for s in starts()]
    two = jnp.concatenate(pieces, axis=0).astype(jnp.bfloat16)
    share = two.shape[0] // len(outs)

    def second(c, first):
        for q in range(0, chunk, 2):
            pieces = [first[k * width : (k + 1) * width] for k in range(q, q + 2)]
            wide = jnp.dot(two, jnp.concatenate(pieces, axis=1), preferred_element_type=jnp.float32)
            for o, out in enumerate(outs):
                for k in range(2):
                    piece = wide[o * share : (o + 1) * share, k * r1 : (k + 1) * r1]
                    out[:, c * chunk + q + k] = piece.reshape(share // TILE, TILE, -1)

    one_copy.wait()
    late = None
    for c in range(chunks):
        copies[c].wait()
        rows = slab_buf[pl.ds(c * chunk, chunk)].reshape(chunk * width, -1)
        middle = rows.shape[1] // 2
        first = jnp.dot(rows[:, :middle], one_buf[:middle], preferred_element_type=jnp.float32)
        first = first + jnp.dot(rows[:, middle:], one_buf[middle:], preferred_element_type=jnp.float32)
        first = first.astype(jnp.bfloat16)
        if late is not None:
            second(c - 1, late)
        late = first
    second(chunks - 1, late)


def project(slab, factor_one, factor_two, starts, outputs):
    depth, width, length = slab.shape
    r1, r2 = factor_one.shape[1], factor_two.shape[1]
    chunk = CHUNK if depth % CHUNK == 0 else 1
    out = pltpu.VMEM((r2 // TILE // outputs, depth, TILE, r1), jnp.float32)
    return pl.pallas_call(
        functools.partial(project_kernel, chunk, starts),
        out_shape=(out,) * outputs,
        in_specs=[pl.BlockSpec(memory_space=pltpu.HBM)] * 3,
        out_specs=[pl.BlockSpec(memory_space=pltpu.VMEM)] * outputs,
        scratch_shapes=[
            pltpu.VMEM(slab.shape, slab.dtype),
            pltpu.VMEM(factor_one.shape, factor_one.dtype),
            pltpu.VMEM(factor_two.shape, factor_two.dtype),
            pltpu.VMEM((r2, width), jnp.float32),
            pltpu.SemaphoreType.DMA((depth // chunk + 2,)),
        ],
        compiler_params=pltpu.CompilerParams(vmem_limit_bytes=32 * 2**20),
        cost_estimate=pl.CostEstimate(
            flops=2 * depth * width * r1 * (length + r2),
            bytes_accessed=2 * (slab.size + factor_one.size) + 4 * depth * r2 * r1,
            transcendentals=0,
        ),
    )(*(pltpu.with_memory_space_constraint(a, pltpu.HBM) for a in (slab, factor_one, factor_two)))


def halves(value):
    high = value.astype(jnp.bfloat16)
    low = (value - high.astype(jnp.float32)).astype(jnp.bfloat16)
    return jnp.concatenate([high, low], axis=0)


def gram_kernel(scale, own_ref, own_add, far_ref, far_add, out_ref, flag_ref, total, gram):
    groups, depth, tile, _ = own_ref.shape
    z, core, x = (lax.axis_index(name) for name in ("z", "core", "col"))
    chips, share, _ = out_ref.shape
    size = depth * tile
    value = jnp.zeros((2 * depth, depth), jnp.float32)
    for g in range(groups):
        total[g, pl.ds(pl.multiple_of(x * size, size), size), :] = (own_ref[g] + own_add[g]).reshape(size, -1)
        total[g, pl.ds(pl.multiple_of((1 - x) * size, size), size), :] = (far_ref[g] + far_add[g]).reshape(size, -1)
    picks = [(g, s) for g in range(groups) for s in range(tile)]
    for n in range(0, len(picks), 16):
        part = picks[n : n + 16]
        rows = jnp.concatenate([total[g, pl.ds(s, 2 * depth, stride=tile), :] for g, s in part], axis=1)
        own = jnp.concatenate([total[g, pl.ds(x * size + s, depth, stride=tile), :] for g, s in part], axis=1)
        four = lax.dot_general(
            halves(rows), halves(own), (((1,), (1,)), ((), ())), preferred_element_type=jnp.float32
        )
        for at in (0, 2 * depth):
            value = value + (four[at : at + 2 * depth, 0:depth] + four[at : at + 2 * depth, depth : 2 * depth])
    gram[:, 0:depth] = value * scale
    for slot, hops in enumerate(((), (SECOND,), (FIRST,), (FIRST, SECOND))):
        to_z = z
        for hop in hops:
            to_z = jnp.bitwise_xor(to_z, hop)
        out_ref[slot] = gram[pl.ds(pl.multiple_of(to_z * share, TILE), share), :]
    flag_ref[...] = jnp.full(flag_ref.shape, core, jnp.int32)


def gram_blocks(own, far, chips, scale):
    groups, depth, tile, r1 = own[0].shape
    full = 2 * depth
    return pl.pallas_call(
        functools.partial(gram_kernel, scale),
        out_shape=(pltpu.VMEM((chips, full // chips, 128), jnp.float32), pltpu.VMEM((TILE, 128), jnp.int32)),
        in_specs=[pl.BlockSpec(memory_space=pltpu.VMEM)] * 4,
        out_specs=[pl.BlockSpec(memory_space=pltpu.VMEM)] * 2,
        scratch_shapes=[
            pltpu.VMEM((groups, full * tile, r1), jnp.float32),
            pltpu.VMEM((full, 128), jnp.float32),
        ],
        cost_estimate=pl.CostEstimate(
            flops=2 * groups * full * depth * tile * r1, bytes_accessed=16 * own[0].size, transcendentals=0
        ),
    )(*(pltpu.with_memory_space_constraint(a, pltpu.VMEM) for a in own + far))


def hop(value, zs, masks, cross=0, flip=0):
    pairs = []
    for z in range(zs):
        for core in range(CORES):
            for x in range(2):
                to = ((z ^ masks[core]) * CORES + (core ^ cross)) * 2 + (x ^ flip)
                pairs.append(((z * CORES + core) * 2 + x, to))
    return lax.ppermute(value, ("z", "core", "col"), pairs)


def swap(value, axis):
    return lax.ppermute(value, axis, [(0, 1), (1, 0)])


FIRST_HOP = (FIRST, SECOND)
SECOND_HOP = (SECOND, FIRST)


def ring_starts(half, width):
    z, core = lax.axis_index("z"), lax.axis_index("core")
    starts = []
    for to_core in (1 - core, core):
        one, two = (to_core * (hops[1] - hops[0]) + hops[0] for hops in (FIRST_HOP, SECOND_HOP))
        for mask in (FIRST ^ SECOND, one, two, 0):
            starts += [to_core * half + jnp.bitwise_xor(z, mask) * width + s for s in range(0, width, TILE)]
    return starts


def ring_plan(zs, scale, slab, factor_one, factor_two):
    half = factor_two.shape[1] // CORES
    starts = functools.partial(ring_starts, half, half // zs)
    parts = project(slab, factor_one, factor_two, starts, 2 * zs)
    passed, given, across, own = (o + swap(t, "core") for t, o in zip(parts[:zs], parts[zs:]))
    arrived = hop(passed, zs, FIRST_HOP)
    beside = hop(given, zs, FIRST_HOP)
    onward = across + arrived
    far_add = hop(onward, zs, SECOND_HOP, flip=1)
    own_add = hop(onward, zs, SECOND_HOP)
    own = lax.optimization_barrier((own, onward))[0] + beside
    blocks, flag = gram_blocks((own, own_add), (swap(own, "col"), far_add), zs, scale)
    blocks = blocks + swap(blocks, "core")
    pair = blocks[:2] + hop(blocks[2:], zs, (FIRST, FIRST), cross=1)
    last = pair[0] + hop(pair[1], zs, (SECOND, SECOND), cross=1)
    depth, rows = slab.shape[0], last.shape[0] // CORES
    return jnp.where(flag[:rows, :depth] == 1, last[rows:, :depth], last[:rows, :depth]).T


def general_plan(scale, slab, factor_one, factor_two):
    depth = slab.shape[0]
    r1, r2 = factor_one.shape[1], factor_two.shape[1]
    half = r2 // CORES

    def starts():
        core = lax.axis_index("core")
        return [side * half + s for side in (1 - core, core) for s in range(0, half, TILE)]

    other, own = project(slab, factor_one, factor_two, starts, 2)
    own = own + swap(other, "core")
    own = own.transpose(0, 2, 1, 3).reshape(half, depth, r1)
    share = lax.psum_scatter(own, "z", scatter_dimension=0, tiled=True)
    whole = lax.all_gather(share, "col", axis=1, tiled=True)
    gram = jnp.einsum("skr,slr->kl", share, whole, precision=lax.Precision.HIGHEST)
    return lax.psum_scatter(gram, ("z", "core"), scatter_dimension=1, tiled=True) * scale


def per_device(zs, cols, slab, factor_one, factor_two):
    r1, r2 = factor_one.shape[1], factor_two.shape[1]
    scale = 1.0 / (r1 * r2)
    depth = slab.shape[0]
    if zs == RING and cols == 2 and r2 % (CORES * zs * TILE) == 0 and cols * depth == zs * TILE:
        return ring_plan(zs, scale, slab, factor_one, factor_two)
    return general_plan(scale, slab, factor_one, factor_two)


def solution(mesh):
    groups, rows, cols = mesh.devices.shape
    zs = rows // CORES
    fine = Mesh(mesh.devices.reshape(groups, zs, CORES, cols), ("groups", "z", "core", "col"))
    row = ("z", "core")
    return jax.shard_map(
        functools.partial(per_device, zs, cols),
        mesh=fine,
        in_specs=(P(("groups", "col"), row, None), P(), P(row, None)),
        out_specs=P(("groups", "col"), row),
        check_vma=False,
    )
```

```python
import functools

import jax
import jax.numpy as jnp
from jax import lax
from jax.experimental import pallas as pl
from jax.experimental.pallas import tpu as pltpu
from jax.sharding import Mesh, PartitionSpec as P

TILE = 8
CORES = 2
CHUNK = 4
RING = 4
FIRST = 1
SECOND = 2


def project_kernel(chunk, starts, slab_ref, one_ref, two_ref, *rest):
    outs, (slab_buf, one_buf, two_buf, turned, sems) = rest[:-5], rest[-5:]
    depth, width, _ = slab_ref.shape
    chunks = depth // chunk
    copies = []
    for c in range(chunks):
        part = pl.ds(c * chunk, chunk)
        copies.append(pltpu.make_async_copy(slab_ref.at[part], slab_buf.at[part], sems.at[c]))
    copies[0].start()
    one_copy = pltpu.make_async_copy(one_ref, one_buf, sems.at[chunks])
    one_copy.start()
    two_copy = pltpu.make_async_copy(two_ref, two_buf, sems.at[chunks + 1])
    two_copy.start()
    for copy in copies[1:]:
        copy.start()
    two_copy.wait()
    turned[...] = two_buf[...].astype(jnp.float32).T
    pieces = [turned[pl.ds(pl.multiple_of(s, TILE), TILE), :] for s in starts()]
    two = jnp.concatenate(pieces, axis=0).astype(jnp.bfloat16)
    share = two.shape[0] // len(outs)

    def second(c, first):
        for q in range(chunk):
            core_part = jnp.dot(two, first[q * width : (q + 1) * width], preferred_element_type=jnp.float32)
            for o, out in enumerate(outs):
                piece = core_part[o * share : (o + 1) * share]
                out[:, c * chunk + q] = piece.reshape(share // TILE, TILE, -1)

    one_copy.wait()
    late = None
    for c in range(chunks):
        copies[c].wait()
        rows = slab_buf[pl.ds(c * chunk, chunk)].reshape(chunk * width, -1)
        middle = rows.shape[1] // 2
        first = jnp.dot(rows[:, :middle], one_buf[:middle], preferred_element_type=jnp.float32)
        first = first + jnp.dot(rows[:, middle:], one_buf[middle:], preferred_element_type=jnp.float32)
        first = first.astype(jnp.bfloat16)
        if late is not None:
            second(c - 1, late)
        late = first
    second(chunks - 1, late)


def project(slab, factor_one, factor_two, starts, outputs):
    depth, width, length = slab.shape
    r1, r2 = factor_one.shape[1], factor_two.shape[1]
    chunk = CHUNK if depth % CHUNK == 0 else 1
    out = pltpu.VMEM((r2 // TILE // outputs, depth, TILE, r1), jnp.float32)
    return pl.pallas_call(
        functools.partial(project_kernel, chunk, starts),
        out_shape=(out,) * outputs,
        in_specs=[pl.BlockSpec(memory_space=pltpu.HBM)] * 3,
        out_specs=[pl.BlockSpec(memory_space=pltpu.VMEM)] * outputs,
        scratch_shapes=[
            pltpu.VMEM(slab.shape, slab.dtype),
            pltpu.VMEM(factor_one.shape, factor_one.dtype),
            pltpu.VMEM(factor_two.shape, factor_two.dtype),
            pltpu.VMEM((r2, width), jnp.float32),
            pltpu.SemaphoreType.DMA((depth // chunk + 2,)),
        ],
        compiler_params=pltpu.CompilerParams(vmem_limit_bytes=32 * 2**20),
        cost_estimate=pl.CostEstimate(
            flops=2 * depth * width * r1 * (length + r2),
            bytes_accessed=2 * (slab.size + factor_one.size) + 4 * depth * r2 * r1,
            transcendentals=0,
        ),
    )(*(pltpu.with_memory_space_constraint(a, pltpu.HBM) for a in (slab, factor_one, factor_two)))


def gram_kernel(scale, own_ref, own_add, far_ref, far_add, out_ref, flag_ref, total):
    groups, depth, tile, _ = own_ref.shape
    z, core, x = (lax.axis_index(name) for name in ("z", "core", "col"))
    chips, share, _ = out_ref.shape
    size = depth * tile
    for g in range(groups):
        total[g, 0:size, :] = (own_ref[g] + own_add[g]).reshape(size, -1)
        total[g, size : 2 * size, :] = (far_ref[g] + far_add[g]).reshape(size, -1)
    picks = [total[g, pl.ds(s, 2 * depth, stride=tile), :] for g in range(groups) for s in range(tile)]
    rows = jnp.concatenate(picks, axis=1)
    high = rows.astype(jnp.bfloat16)
    low = (rows - high.astype(jnp.float32)).astype(jnp.bfloat16)
    four = lax.dot_general(
        jnp.concatenate([high, low], axis=0),
        jnp.concatenate([high[0:depth], low[0:depth]], axis=0),
        (((1,), (1,)), ((), ())),
        preferred_element_type=jnp.float32,
    )
    value = (four[0 : 2 * depth, 0:depth] + four[0 : 2 * depth, depth : 2 * depth]) + (
        four[2 * depth : 4 * depth, 0:depth] + four[2 * depth : 4 * depth, depth : 2 * depth]
    )
    value = value * scale
    for n in range(chips):
        half, part = n // 2, n % 2
        mask = jnp.bitwise_xor(z, 2 * (x if half == 0 else 1 - x) + part)
        slot = mask // SECOND + 2 * (mask % SECOND)
        out_ref[slot, :, 0:depth] = value[n * share : (n + 1) * share]
    flag_ref[...] = jnp.full(flag_ref.shape, core, jnp.int32)


def gram_blocks(own, far, chips, scale):
    groups, depth, tile, r1 = own[0].shape
    full = 2 * depth
    return pl.pallas_call(
        functools.partial(gram_kernel, scale),
        out_shape=(pltpu.VMEM((chips, full // chips, 128), jnp.float32), pltpu.VMEM((TILE, 128), jnp.int32)),
        in_specs=[pl.BlockSpec(memory_space=pltpu.VMEM)] * 4,
        out_specs=[pl.BlockSpec(memory_space=pltpu.VMEM)] * 2,
        scratch_shapes=[
            pltpu.VMEM((groups, full * tile, r1), jnp.float32),
        ],
        cost_estimate=pl.CostEstimate(
            flops=2 * groups * full * depth * tile * r1, bytes_accessed=16 * own[0].size, transcendentals=0
        ),
    )(*(pltpu.with_memory_space_constraint(a, pltpu.VMEM) for a in own + far))


def hop(value, zs, masks, cross=0, flip=0):
    pairs = []
    for z in range(zs):
        for core in range(CORES):
            for x in range(2):
                to = ((z ^ masks[core]) * CORES + (core ^ cross)) * 2 + (x ^ flip)
                pairs.append(((z * CORES + core) * 2 + x, to))
    return lax.ppermute(value, ("z", "core", "col"), pairs)


def swap(value, axis):
    return lax.ppermute(value, axis, [(0, 1), (1, 0)])


FIRST_HOP = (FIRST, SECOND)
SECOND_HOP = (SECOND, FIRST)


def ring_starts(half, width):
    z, core = lax.axis_index("z"), lax.axis_index("core")
    starts = []
    for to_core in (1 - core, core):
        one, two = (to_core * (hops[1] - hops[0]) + hops[0] for hops in (FIRST_HOP, SECOND_HOP))
        for mask in (FIRST ^ SECOND, one, two, 0):
            starts += [to_core * half + jnp.bitwise_xor(z, mask) * width + s for s in range(0, width, TILE)]
    return starts


def ring_plan(zs, scale, slab, factor_one, factor_two):
    half = factor_two.shape[1] // CORES
    starts = functools.partial(ring_starts, half, half // zs)
    parts = project(slab, factor_one, factor_two, starts, 2 * zs)
    passed, given, across, own = (o + swap(t, "core") for t, o in zip(parts[:zs], parts[zs:]))
    arrived = hop(passed, zs, FIRST_HOP)
    beside = hop(given, zs, FIRST_HOP)
    onward = across + arrived
    far_add = hop(onward, zs, SECOND_HOP, flip=1)
    own_add = hop(onward, zs, SECOND_HOP)
    own = lax.optimization_barrier((own, onward))[0] + beside
    blocks, flag = gram_blocks((own, own_add), (swap(own, "col"), far_add), zs, scale)
    blocks = blocks + swap(blocks, "core")
    pair = blocks[:2] + hop(blocks[2:], zs, (FIRST, FIRST), cross=1)
    last = pair[0] + hop(pair[1], zs, (SECOND, SECOND), cross=1)
    depth, rows = slab.shape[0], last.shape[0] // CORES
    return jnp.where(flag[:rows, :depth] == 1, last[rows:, :depth], last[:rows, :depth]).T


def general_plan(scale, slab, factor_one, factor_two):
    depth = slab.shape[0]
    r1, r2 = factor_one.shape[1], factor_two.shape[1]
    half = r2 // CORES

    def starts():
        core = lax.axis_index("core")
        return [side * half + s for side in (1 - core, core) for s in range(0, half, TILE)]

    other, own = project(slab, factor_one, factor_two, starts, 2)
    own = own + swap(other, "core")
    own = own.transpose(0, 2, 1, 3).reshape(half, depth, r1)
    share = lax.psum_scatter(own, "z", scatter_dimension=0, tiled=True)
    whole = lax.all_gather(share, "col", axis=1, tiled=True)
    gram = jnp.einsum("skr,slr->kl", share, whole, precision=lax.Precision.HIGHEST)
    return lax.psum_scatter(gram, ("z", "core"), scatter_dimension=1, tiled=True) * scale


def per_device(zs, cols, slab, factor_one, factor_two):
    r1, r2 = factor_one.shape[1], factor_two.shape[1]
    scale = 1.0 / (r1 * r2)
    depth = slab.shape[0]
    if zs == RING and cols == 2 and r2 % (CORES * zs * TILE) == 0 and cols * depth == zs * TILE:
        return ring_plan(zs, scale, slab, factor_one, factor_two)
    return general_plan(scale, slab, factor_one, factor_two)


def solution(mesh):
    groups, rows, cols = mesh.devices.shape
    zs = rows // CORES
    fine = Mesh(mesh.devices.reshape(groups, zs, CORES, cols), ("groups", "z", "core", "col"))
    row = ("z", "core")
    return jax.shard_map(
        functools.partial(per_device, zs, cols),
        mesh=fine,
        in_specs=(P(("groups", "col"), row, None), P(), P(row, None)),
        out_specs=P(("groups", "col"), row),
        check_vma=False,
    )
```

```python
import functools

import jax
import jax.numpy as jnp
from jax import lax
from jax.experimental import pallas as pl
from jax.experimental.pallas import tpu as pltpu
from jax.sharding import Mesh, PartitionSpec as P

TILE = 8
CORES = 2
CHUNK = 4
RING = 4
FIRST = 1
SECOND = 2


def project_kernel(chunk, starts, slab_ref, one_ref, two_ref, *rest):
    outs, (slab_buf, one_buf, two_buf, turned, sems) = rest[:-5], rest[-5:]
    depth, width, _ = slab_ref.shape
    chunks = depth // chunk
    copies = []
    for c in range(chunks):
        part = pl.ds(c * chunk, chunk)
        copies.append(pltpu.make_async_copy(slab_ref.at[part], slab_buf.at[part], sems.at[c]))
    copies[0].start()
    one_copy = pltpu.make_async_copy(one_ref, one_buf, sems.at[chunks])
    one_copy.start()
    two_copy = pltpu.make_async_copy(two_ref, two_buf, sems.at[chunks + 1])
    two_copy.start()
    for copy in copies[1:]:
        copy.start()
    two_copy.wait()
    turned[...] = two_buf[...].astype(jnp.float32).T
    pieces = [turned[pl.ds(pl.multiple_of(s, TILE), TILE), :] for s in starts()]
    two = jnp.concatenate(pieces, axis=0).astype(jnp.bfloat16)
    share = two.shape[0] // len(outs)

    def second(c, first):
        for q in range(chunk):
            core_part = jnp.dot(two, first[q * width : (q + 1) * width], preferred_element_type=jnp.float32)
            for o, out in enumerate(outs):
                piece = core_part[o * share : (o + 1) * share]
                out[:, c * chunk + q] = piece.reshape(share // TILE, TILE, -1)

    one_copy.wait()
    late = None
    for c in range(chunks):
        copies[c].wait()
        rows = slab_buf[pl.ds(c * chunk, chunk)].reshape(chunk * width, -1)
        middle = rows.shape[1] // 2
        first = jnp.dot(rows[:, :middle], one_buf[:middle], preferred_element_type=jnp.float32)
        first = first + jnp.dot(rows[:, middle:], one_buf[middle:], preferred_element_type=jnp.float32)
        first = first.astype(jnp.bfloat16)
        if late is not None:
            second(c - 1, late)
        late = first
    second(chunks - 1, late)


def project(slab, factor_one, factor_two, starts, outputs):
    depth, width, length = slab.shape
    r1, r2 = factor_one.shape[1], factor_two.shape[1]
    chunk = CHUNK if depth % CHUNK == 0 else 1
    out = pltpu.VMEM((r2 // TILE // outputs, depth, TILE, r1), jnp.float32)
    return pl.pallas_call(
        functools.partial(project_kernel, chunk, starts),
        out_shape=(out,) * outputs,
        in_specs=[pl.BlockSpec(memory_space=pltpu.HBM)] * 3,
        out_specs=[pl.BlockSpec(memory_space=pltpu.VMEM)] * outputs,
        scratch_shapes=[
            pltpu.VMEM(slab.shape, slab.dtype),
            pltpu.VMEM(factor_one.shape, factor_one.dtype),
            pltpu.VMEM(factor_two.shape, factor_two.dtype),
            pltpu.VMEM((r2, width), jnp.float32),
            pltpu.SemaphoreType.DMA((depth // chunk + 2,)),
        ],
        compiler_params=pltpu.CompilerParams(vmem_limit_bytes=32 * 2**20),
        cost_estimate=pl.CostEstimate(
            flops=2 * depth * width * r1 * (length + r2),
            bytes_accessed=2 * (slab.size + factor_one.size) + 4 * depth * r2 * r1,
            transcendentals=0,
        ),
    )(*(pltpu.with_memory_space_constraint(a, pltpu.HBM) for a in (slab, factor_one, factor_two)))


def halves(value):
    high = value.astype(jnp.bfloat16)
    low = (value - high.astype(jnp.float32)).astype(jnp.bfloat16)
    return jnp.concatenate([high, low], axis=0)


def gram_kernel(scale, own_ref, own_add, far_ref, far_add, out_ref, flag_ref, total, gram):
    groups, depth, tile, _ = own_ref.shape
    z, core, x = (lax.axis_index(name) for name in ("z", "core", "col"))
    chips, share, _ = out_ref.shape
    size = depth * tile
    value = jnp.zeros((2 * depth, depth), jnp.float32)
    for g in range(groups):
        total[g, pl.ds(pl.multiple_of(x * size, size), size), :] = (own_ref[g] + own_add[g]).reshape(size, -1)
        total[g, pl.ds(pl.multiple_of((1 - x) * size, size), size), :] = (far_ref[g] + far_add[g]).reshape(size, -1)
    picks = [(g, s) for g in range(groups) for s in range(tile)]
    for n in range(0, len(picks), 4):
        part = picks[n : n + 4]
        rows = jnp.concatenate([total[g, pl.ds(s, 2 * depth, stride=tile), :] for g, s in part], axis=1)
        own = jnp.concatenate([total[g, pl.ds(x * size + s, depth, stride=tile), :] for g, s in part], axis=1)
        four = lax.dot_general(
            halves(rows), halves(own), (((1,), (1,)), ((), ())), preferred_element_type=jnp.float32
        )
        for at in (0, 2 * depth):
            value = value + (four[at : at + 2 * depth, 0:depth] + four[at : at + 2 * depth, depth : 2 * depth])
    gram[:, 0:depth] = value * scale
    for slot, hops in enumerate(((), (SECOND,), (FIRST,), (FIRST, SECOND))):
        to_z = z
        for hop in hops:
            to_z = jnp.bitwise_xor(to_z, hop)
        out_ref[slot] = gram[pl.ds(pl.multiple_of(to_z * share, TILE), share), :]
    flag_ref[...] = jnp.full(flag_ref.shape, core, jnp.int32)


def gram_blocks(own, far, chips, scale):
    groups, depth, tile, r1 = own[0].shape
    full = 2 * depth
    return pl.pallas_call(
        functools.partial(gram_kernel, scale),
        out_shape=(pltpu.VMEM((chips, full // chips, 128), jnp.float32), pltpu.VMEM((TILE, 128), jnp.int32)),
        in_specs=[pl.BlockSpec(memory_space=pltpu.VMEM)] * 4,
        out_specs=[pl.BlockSpec(memory_space=pltpu.VMEM)] * 2,
        scratch_shapes=[
            pltpu.VMEM((groups, full * tile, r1), jnp.float32),
            pltpu.VMEM((full, 128), jnp.float32),
        ],
        cost_estimate=pl.CostEstimate(
            flops=2 * groups * full * depth * tile * r1, bytes_accessed=16 * own[0].size, transcendentals=0
        ),
    )(*(pltpu.with_memory_space_constraint(a, pltpu.VMEM) for a in own + far))


def hop(value, zs, masks, cross=0, flip=0):
    pairs = []
    for z in range(zs):
        for core in range(CORES):
            for x in range(2):
                to = ((z ^ masks[core]) * CORES + (core ^ cross)) * 2 + (x ^ flip)
                pairs.append(((z * CORES + core) * 2 + x, to))
    return lax.ppermute(value, ("z", "core", "col"), pairs)


def swap(value, axis):
    return lax.ppermute(value, axis, [(0, 1), (1, 0)])


FIRST_HOP = (FIRST, SECOND)
SECOND_HOP = (SECOND, FIRST)


def ring_starts(half, width):
    z, core = lax.axis_index("z"), lax.axis_index("core")
    starts = []
    for to_core in (1 - core, core):
        one, two = (to_core * (hops[1] - hops[0]) + hops[0] for hops in (FIRST_HOP, SECOND_HOP))
        for mask in (FIRST ^ SECOND, one, two, 0):
            starts += [to_core * half + jnp.bitwise_xor(z, mask) * width + s for s in range(0, width, TILE)]
    return starts


def ring_plan(zs, scale, slab, factor_one, factor_two):
    half = factor_two.shape[1] // CORES
    starts = functools.partial(ring_starts, half, half // zs)
    parts = project(slab, factor_one, factor_two, starts, 2 * zs)
    passed, given, across, own = (o + swap(t, "core") for t, o in zip(parts[:zs], parts[zs:]))
    arrived = hop(passed, zs, FIRST_HOP)
    beside = hop(given, zs, FIRST_HOP)
    onward = across + arrived
    far_add = hop(onward, zs, SECOND_HOP, flip=1)
    own_add = hop(onward, zs, SECOND_HOP)
    own = lax.optimization_barrier((own, onward))[0] + beside
    blocks, flag = gram_blocks((own, own_add), (swap(own, "col"), far_add), zs, scale)
    blocks = blocks + swap(blocks, "core")
    pair = blocks[:2] + hop(blocks[2:], zs, (FIRST, FIRST), cross=1)
    last = pair[0] + hop(pair[1], zs, (SECOND, SECOND), cross=1)
    depth, rows = slab.shape[0], last.shape[0] // CORES
    return jnp.where(flag[:rows, :depth] == 1, last[rows:, :depth], last[:rows, :depth]).T


def general_plan(scale, slab, factor_one, factor_two):
    depth = slab.shape[0]
    r1, r2 = factor_one.shape[1], factor_two.shape[1]
    half = r2 // CORES

    def starts():
        core = lax.axis_index("core")
        return [side * half + s for side in (1 - core, core) for s in range(0, half, TILE)]

    other, own = project(slab, factor_one, factor_two, starts, 2)
    own = own + swap(other, "core")
    own = own.transpose(0, 2, 1, 3).reshape(half, depth, r1)
    share = lax.psum_scatter(own, "z", scatter_dimension=0, tiled=True)
    whole = lax.all_gather(share, "col", axis=1, tiled=True)
    gram = jnp.einsum("skr,slr->kl", share, whole, precision=lax.Precision.HIGHEST)
    return lax.psum_scatter(gram, ("z", "core"), scatter_dimension=1, tiled=True) * scale


def per_device(zs, cols, slab, factor_one, factor_two):
    r1, r2 = factor_one.shape[1], factor_two.shape[1]
    scale = 1.0 / (r1 * r2)
    depth = slab.shape[0]
    if zs == RING and cols == 2 and r2 % (CORES * zs * TILE) == 0 and cols * depth == zs * TILE:
        return ring_plan(zs, scale, slab, factor_one, factor_two)
    return general_plan(scale, slab, factor_one, factor_two)


def solution(mesh):
    groups, rows, cols = mesh.devices.shape
    zs = rows // CORES
    fine = Mesh(mesh.devices.reshape(groups, zs, CORES, cols), ("groups", "z", "core", "col"))
    row = ("z", "core")
    return jax.shard_map(
        functools.partial(per_device, zs, cols),
        mesh=fine,
        in_specs=(P(("groups", "col"), row, None), P(), P(row, None)),
        out_specs=P(("groups", "col"), row),
        check_vma=False,
    )
```
